32 devices in a mesh: gx: 2 (over x), gy: 4 (over z), gz: 4 (over y, core).
Axes of the slice: x: 2, y: 2, z: 4, core: 2. Of those that a mesh axis runs over, the one named last changes fastest.
Arguments:
- checkpoint: float32 [64, 256, 1024], P('gx', 'gy', 'gz'), may hold values from -6 to 6
- diffusivity: float32 [64, 256, 1024], P('gx', 'gy', 'gz'), may hold values from 0.1 to 1
- material_scale: float32 [4], replicated, may hold values from 0.5 to 1
- labels: int32 [64, 256, 1024], P('gx', 'gy', 'gz'), may hold values from 0 to 3
- measured: float32 [64, 256, 1024], P('gx', 'gy', 'gz'), may hold values from -6 to 6
- observed: int32 [64, 256, 1024], P('gx', 'gy', 'gz'), may hold values 0 or 1
- adjoint_in: float32 [64, 256, 1024], P('gx', 'gy', 'gz'), may hold values from -4 to 4
Outputs:
- gradient: float32 [64, 256, 1024], P('gx', 'gy', 'gz')
- adjoint_start: float32 [64, 256, 1024], P('gx', 'gy', 'gz')
The draws below stay inside these ranges and needn't reach their ends.
All inputs are finite; a program needn't handle non-finite values. No bound on the sum of `observed` on one device may be relied on, other than what follows from the above.
Results may differ from the reference program's by a relative error of at most 0.00002.
Values sent between devices are 32-bit elements; how exact they have to be, the bound alone decides.
No kernel may reach another device: no remote copies, remote signals or barrier semaphores. Data moves between devices by JAX's collectives and lax.ppermute only.
A program may use at most 192 MiB of HBM per device.

```python
import math
import jax
import jax.numpy as jnp

ITERS = 4
MATERIALS = 4
NX = 64
NY = 256
NZ = 1024


def place_ends(values, stream_key, smallest, high):
    longest = values.shape.index(max(values.shape))
    spots = []
    for shift in (0, 1):
        where = [jax.random.randint(jax.random.fold_in(stream_key, axis), (), 0, length) for axis, length in enumerate(values.shape)]
        where[longest] = (where[longest] + shift) % values.shape[longest]
        spots.append(tuple(where))
    return values.at[spots[0]].set(smallest).at[spots[1]].set(high)


def level_of(key, dims, cuts, low, top_value):
    factor_of, own = 1.0, jax.random.fold_in(key, 6)
    for axis_at, blocks in cuts:
        heights = jnp.exp(jax.random.uniform(jax.random.fold_in(own, axis_at), (blocks,), jnp.float32, low / len(cuts), top_value / len(cuts)))
        factor_of = factor_of * jnp.repeat(heights, dims[axis_at] // blocks).reshape([-1 if axis == axis_at else 1 for axis in range(len(dims))])
    return factor_of


def noise(stream_key, shape, scale, reach, cuts=(), held_as=jnp.bfloat16):
    factor_of = level_of(stream_key, shape, cuts, -0.22, 0.18) if cuts else 1.0
    drawn = jax.random.normal(stream_key, shape, jnp.float32) * scale * factor_of
    return jnp.minimum(jnp.maximum(drawn, -reach), reach).astype(held_as)


def setup_inputs(seed: int = 0) -> dict:
    streams_of = jax.random.split(jax.random.key(seed), 8)
    return {
        "checkpoint": noise(streams_of[0], (NX, NY, NZ), 1.0, 6.0, ((0, 2), (1, 4), (2, 4)), jnp.float32),
        "diffusivity": jnp.clip(jnp.exp(math.log(1.0) - 2.3025851 * jax.random.uniform(streams_of[1], (NX, NY, NZ), jnp.float32) ** level_of(streams_of[1], (NX, NY, NZ), ((0, 2), (1, 4), (2, 4)), -0.2, 0.2)), 0.1, 1.0),
        "material_scale": jnp.clip(jax.random.uniform(streams_of[2], (MATERIALS,), jnp.float32, 0.5, 1.0), 0.5, 1.0),
        "labels": place_ends(jax.random.randint(streams_of[3], (NX, NY, NZ), 0, MATERIALS), jax.random.fold_in(streams_of[3], 1), 0, MATERIALS - 1).astype(jnp.int32),
        "measured": noise(streams_of[4], (NX, NY, NZ), 1.0, 6.0, ((0, 2), (1, 4), (2, 4)), jnp.float32),
        "observed": place_ends((jax.random.randint(streams_of[5], (NX, NY, NZ), 0, 2) < 1).astype(jnp.int32), jax.random.fold_in(streams_of[5], 1), 0, 1),
        "adjoint_in": noise(streams_of[6], (NX, NY, NZ), 0.5, 4.0, ((0, 2), (1, 4), (2, 4)), jnp.float32),
    }


RATE = 0.15


def neighbour(x, dim, off):
    parts = [slice(1, -1), slice(1, -1), slice(1, -1)]
    parts[dim] = slice(off, x.shape[dim] - 2 + off)
    return x[tuple(parts)]


def advance(field_pad, kappa_pad):
    centre = neighbour(field_pad, 0, 1)
    kcentre = neighbour(kappa_pad, 0, 1)
    total = jnp.zeros_like(centre)
    for dim in range(3):
        for off in (0, 2):
            total = total + 0.5 * (kcentre + neighbour(kappa_pad, dim, off)) * (neighbour(field_pad, dim, off) - centre)
    return centre + RATE * total


def grad_term(lam_pad, temp_pad):
    lcentre = neighbour(lam_pad, 0, 1)
    tcentre = neighbour(temp_pad, 0, 1)
    total = jnp.zeros_like(lcentre)
    for dim in range(3):
        for off in (0, 2):
            total = total + (neighbour(lam_pad, dim, off) - lcentre) * (neighbour(temp_pad, dim, off) - tcentre)
    return -0.5 * RATE * total


def reference(checkpoint, diffusivity, material_scale, labels, measured, observed, adjoint_in):
    factor = material_scale[labels]
    kappa_pad = jnp.pad(diffusivity * factor, 1)
    history = []
    temp = checkpoint
    for step in range(ITERS):
        history.append(temp)
        temp = advance(jnp.pad(temp, 1), kappa_pad)
    lam = adjoint_in + observed.astype(jnp.float32) * (temp - measured)
    acc = jnp.zeros_like(checkpoint)
    for step in range(ITERS - 1, -1, -1):
        lam_pad = jnp.pad(lam, 1)
        acc = acc + grad_term(lam_pad, jnp.pad(history[step], 1))
        lam = advance(lam_pad, kappa_pad)
    return acc * factor, lam
```

```python
import functools

import jax
import jax.numpy as jnp
from jax import lax
from jax.experimental import pallas as pl
from jax.experimental.pallas import tpu as pltpu
from jax.sharding import PartitionSpec as P

ITERS = 4
MATERIALS = 4
HALO = ITERS
HALF_RATE = 0.5 * 0.15
ROWS = 80
OWN = 8
GROUPS = 4
BLOCK = 128 // GROUPS
F32 = jnp.float32

in_vmem = pl.BlockSpec(memory_space=pltpu.VMEM)
in_smem = pl.BlockSpec(memory_space=pltpu.SMEM)


def params():
    return pltpu.CompilerParams(vmem_limit_bytes=12 << 20)


def vm(*shape):
    return pltpu.VMEM(shape, F32)


def lanes():
    return lax.broadcasted_iota(jnp.int32, (8, 128), 1)


def sublanes():
    return lax.broadcasted_iota(jnp.int32, (8, 128), 0)


def each(fn, *lists):
    return [fn(*items) for items in zip(*lists)]


def add(a, b):
    return each(lambda x, y: x + y, a, b)


def sub(a, b):
    return each(lambda x, y: x - y, a, b)


def mul(a, b):
    return each(lambda x, y: x * y, a, b)


def load(ref, x, row, tiles):
    return [ref[x * tiles + t, pl.ds(row, 8), :] for t in range(tiles)]


def store(ref, x, row, values):
    for t, value in enumerate(values):
        ref[x * len(values) + t, pl.ds(row, 8), :] = value


def ahead(values):
    rolled = [pltpu.roll(v, 127, axis=1) for v in values]
    count = len(values)
    if count == 1:
        return rolled
    last = lanes() == 127
    return [jnp.where(last, rolled[(t + 1) % count], rolled[t]) for t in range(count)]


def behind(values):
    rolled = [pltpu.roll(v, 1, axis=1) for v in values]
    count = len(values)
    if count == 1:
        return rolled
    first = lanes() == 0
    return [jnp.where(first, rolled[(t - 1) % count], rolled[t]) for t in range(count)]


class Plan:
    def __init__(self, mesh, shape):
        self.sizes = {axis: mesh.shape[axis] for axis in ("gx", "gy", "gz")}
        self.nx = shape[0] // self.sizes["gx"]
        self.ny = shape[1] // self.sizes["gy"]
        self.nz = shape[2] // self.sizes["gz"]
        self.tiles = self.nz // 128
        self.two_sided = self.sizes["gx"] > 2
        self.deep = self.nx + HALO * (2 if self.two_sided else 1)
        self.planes = self.deep + 2
        self.per_group = self.deep // GROUPS
        self.edge_planes = self.per_group + 2
        self.row_tiles = [OWN - HALO + 8 * t for t in range((self.ny + 2 * HALO) // 8)]
        self.own_tiles = [OWN + 8 * t for t in range(self.ny // 8)]
        self.unroll = 4 if self.two_sided else 3
        self.edge_vregs = self.per_group * len(self.row_tiles)
        self.face_vregs = -(-self.edge_vregs // 4)

    def index(self, axis):
        return lax.axis_index(axis)

    def even(self, axis):
        return lax.rem(lax.axis_index(axis), 2) == 0

    def first(self, axis):
        return lax.axis_index(axis) == 0

    def last(self, axis):
        return lax.axis_index(axis) == self.sizes[axis] - 1

    def own_plane(self):
        if self.two_sided:
            return jnp.int32(1 + HALO)
        return jnp.where(self.even("gx"), 1, 1 + HALO)

    def span(self, step):
        unroll = self.unroll
        if step == ITERS - 1 and self.two_sided:
            return self.own_plane(), self.nx
        if self.two_sided:
            return 1, self.deep
        need = self.nx + HALO - 1 - step
        count = -(-need // unroll) * unroll
        return jnp.where(self.even("gx"), 1, 1 + self.deep - count), count

    def row_keep(self, row):
        if row < OWN:
            return (sublanes() >= OWN - row) | jnp.logical_not(self.first("gy"))
        if row + 8 > OWN + self.ny:
            return (sublanes() < OWN + self.ny - row) | jnp.logical_not(self.last("gy"))
        return None

    def edge_keep(self):
        pos = lanes() % BLOCK
        low = (pos >= 16) & (pos < 20) & self.first("gz")
        high = (pos >= 12) & (pos < 16) & self.last("gz")
        return jnp.logical_not(low | high)


def pairs(count, second):
    if not second:
        return [(i, i ^ 1) for i in range(count)]
    inner = [(i, i + 1) for i in range(1, count - 1, 2)]
    return inner + [(b, a) for a, b in inner]


def swap(plan, axis, first, second, wrap):
    count = plan.sizes[axis]
    got = lax.ppermute(first, axis, pairs(count, False))
    if count == 2:
        return got, got
    ends = [(0, count - 1), (count - 1, 0)] if wrap else [(0, 0), (count - 1, count - 1)]
    return got, lax.ppermute(second, axis, pairs(count, True) + ends)


def send_faces(plan, fields, px, px2, pya, pyb):
    nt = plan.tiles
    own = plan.own_plane()
    even_x, even_y = plan.even("gx"), plan.even("gy")
    wide = HALO * nt
    rows = pl.ds(OWN, plan.ny)
    low, high = own * nt, (own + plan.nx - HALO) * nt
    for f, field in enumerate(fields):
        at = jnp.where(even_x, high, low)
        for j in range(wide):
            px[f * wide + j] = field[at + j, rows, :]
        if plan.two_sided:
            at = jnp.where(even_x, low, high)
            for j in range(wide):
                px2[f * wide + j] = field[at + j, rows, :]
    top = OWN + plan.ny - HALO

    def body(x, _):
        for f, field in enumerate(fields):
            for t in range(nt):
                a = field[(own + x) * nt + t, pl.ds(OWN, HALO), :]
                b = field[(own + x) * nt + t, pl.ds(top, HALO), :]
                if len(fields) == 2:
                    to = (x * nt + t, pl.ds(HALO * f, HALO))
                else:
                    to = (x * (nt // 2) + t // 2, pl.ds(HALO * (t % 2), HALO))
                pya[to[0], to[1], :] = jnp.where(even_y, b, a)
                pyb[to[0], to[1], :] = jnp.where(even_y, a, b)
        return 0

    lax.fori_loop(0, plan.nx, body, 0, unroll=4)


def corner_kernel(plan, per, ya, yb, out, out2):
    even = plan.even("gx")
    low, high = 0, (plan.nx - HALO) * per
    width = HALO * per
    at = jnp.where(even, high, low)
    for n, ref in enumerate((ya, yb)):
        out[n * width : (n + 1) * width] = ref[pl.ds(at, width)]
    if plan.two_sided:
        at = jnp.where(even, low, high)
        for n, ref in enumerate((ya, yb)):
            out2[n * width : (n + 1) * width] = ref[pl.ds(at, width)]


def place_halos(plan, fields, xa, xb, ya, yb, ca, cb):
    nt = plan.tiles
    own = plan.own_plane()
    wide = HALO * nt
    even_x, even_y = plan.even("gx"), plan.even("gy")
    two = len(fields) == 2
    per = nt if two else nt // 2
    below, above = own - HALO, own + plan.nx
    rows = pl.ds(OWN, plan.ny)

    def put_rows(plane, source_a, source_b, at, blank):
        for f, field in enumerate(fields):
            for t in range(nt):
                if two:
                    a = source_a[at + t, pl.ds(HALO * f, HALO), :]
                    b = source_b[at + t, pl.ds(HALO * f, HALO), :]
                else:
                    a = source_a[at + t // 2, pl.ds(HALO * (t % 2), HALO), :]
                    b = source_b[at + t // 2, pl.ds(HALO * (t % 2), HALO), :]
                low = jnp.where(even_y, b, a)
                high = jnp.where(even_y, a, b)
                low = jnp.where(plan.first("gy") | blank, 0.0, low)
                high = jnp.where(plan.last("gy") | blank, 0.0, high)
                field[plane * nt + t, pl.ds(OWN - HALO, HALO), :] = low
                field[plane * nt + t, pl.ds(OWN + plan.ny, HALO), :] = high

    def body(x, _):
        put_rows(own + x, ya, yb, x * per, False)
        return 0

    lax.fori_loop(0, plan.nx, body, 0, unroll=4)

    sides = [(xa, ca, jnp.where(even_x, above, below), False)]
    if plan.two_sided:
        sides[0] = (xa, ca, jnp.where(even_x, above, below), False)
        ends = (even_x & plan.first("gx")) | (jnp.logical_not(even_x) & plan.last("gx"))
        sides.append((xb, cb, jnp.where(even_x, below, above), ends))
    for x_ref, c_ref, plane, blank in sides:
        for f, field in enumerate(fields):
            for j in range(wide):
                value = x_ref[f * wide + j]
                if blank is not False:
                    value = jnp.where(blank, 0.0, value)
                field[plane * nt + j, rows, :] = value
        half = HALO * per
        for j in range(HALO):
            put_rows(plane + j, c_ref.at[pl.ds(0, half)], c_ref.at[pl.ds(half, half)], j * per, blank)
    zero = jnp.zeros((ROWS, 128), F32)
    for field in fields:
        for t in range(nt):
            field[t] = zero
            field[(plan.planes - 1) * nt + t] = zero


def pack_edges(plan, field, edge, row_tiles):
    nt = plan.tiles
    masks = [lanes() >= 16 * j for j in range(2 * GROUPS)]

    def body(i, _):
        for row in row_tiles:
            value = None
            for g in range(GROUPS):
                plane = (g * plan.per_group + 1 + i) * nt
                right = pltpu.roll(field[plane + nt - 1, pl.ds(row, 8), :], (BLOCK * g + 12) % 128, axis=1)
                left = pltpu.roll(field[plane, pl.ds(row, 8), :], (BLOCK * g + 20) % 128, axis=1)
                value = right if value is None else jnp.where(masks[2 * g], right, value)
                value = jnp.where(masks[2 * g + 1], left, value)
            edge[i + 1, pl.ds(row, 8), :] = value
        return 0

    lax.fori_loop(0, plan.per_group, body, 0)


def edge_places(plan):
    return [(i + 1, row) for i in range(plan.per_group) for row in plan.row_tiles]


def pack_faces(plan, edge, out, base):
    lane = lanes()
    places = edge_places(plan)
    for q in range(plan.face_vregs):
        value = None
        for slot, (i, row) in enumerate(places[4 * q : 4 * q + 4]):
            held = edge[i, pl.ds(row, 8), :]
            low = pltpu.roll(held, (8 * slot - 20) % 128, axis=1)
            high = pltpu.roll(held, (8 * slot - 4) % 128, axis=1)
            both = jnp.where(lane % 8 < 4, low, high)
            value = both if value is None else jnp.where(lane % BLOCK >= 8 * slot, both, value)
        out[base + q] = value


def place_faces(plan, edge, za, zb, base):
    lane = lanes()
    pos = lane % BLOCK
    halo = (pos >= 12) & (pos < 20)
    even = plan.even("gz")
    places = edge_places(plan)
    for q in range(plan.face_vregs):
        a, b = za[base + q], zb[base + q]
        right = jnp.where(plan.last("gz"), 0.0, jnp.where(even, a, b))
        left = jnp.where(plan.first("gz"), 0.0, jnp.where(even, b, a))
        both = jnp.where(lane % 8 < 4, right, left)
        for slot, (i, row) in enumerate(places[4 * q : 4 * q + 4]):
            moved = pltpu.roll(both, (12 - 8 * slot) % 128, axis=1)
            edge[i, pl.ds(row, 8), :] = jnp.where(halo, moved, edge[i, pl.ds(row, 8), :])


def wrap_planes(plan, edge):
    lane = lanes()
    last = plan.per_group
    for row in plan.row_tiles:
        before = pltpu.roll(edge[last, pl.ds(row, 8), :], BLOCK, axis=1)
        after = pltpu.roll(edge[1, pl.ds(row, 8), :], 128 - BLOCK, axis=1)
        edge[0, pl.ds(row, 8), :] = jnp.where(lane < BLOCK, 0.0, before)
        edge[last + 1, pl.ds(row, 8), :] = jnp.where(lane >= 128 - BLOCK, 0.0, after)


def merge_edges(plan, values, edge, plane, row):
    lane = lanes()
    g = (plane - 1) // plan.per_group
    i = plane - g * plan.per_group
    held = edge[i, pl.ds(row, 8), :]
    left = pltpu.roll(held, lax.rem(256 - 20 - BLOCK * g, 128), axis=1)
    right = pltpu.roll(held, lax.rem(256 - 12 - BLOCK * g, 128), axis=1)
    values = list(values)
    values[0] = jnp.where(lane < 4, left, values[0])
    values[-1] = jnp.where(lane >= 124, right, values[-1])
    return values


def face_coefficients(plan, k, cx, cy, cz, czm, planes, tiles):
    def body(x, _):
        for row in plan.row_tiles:
            here = load(k, x, row, tiles)
            store(cx, x, row, add(here, load(k, x + 1, row, tiles)))
            store(cy, x, row, add(here, load(k, x, row + 1, tiles)))
            store(cz, x, row, add(here, ahead(here)))
            store(czm, x, row, add(here, behind(here)))
        return 0

    lax.fori_loop(0, planes - 1, body, 0, unroll=2)


def step_forward(plan, v, w, c, start, count, unroll, row_tiles, tiles, keep, plane_keep):
    cx, cy, cz, czm = c

    def body(i, _):
        first = start + i * unroll
        for row in row_tiles:
            here = load(v, first, row, tiles)
            flow = mul(load(cx, first - 1, row, tiles), sub(here, load(v, first - 1, row, tiles)))
            for k in range(unroll):
                x = first + k
                after = load(v, x + 1, row, tiles)
                out = mul(load(cx, x, row, tiles), sub(after, here))
                total = add(here, sub(out, flow))
                flow = out
                up = mul(load(cy, x, row, tiles), sub(load(v, x, row + 1, tiles), here))
                down = mul(load(cy, x, row - 1, tiles), sub(here, load(v, x, row - 1, tiles)))
                total = add(total, sub(up, down))
                right = mul(load(cz, x, row, tiles), sub(ahead(here), here))
                left = mul(load(czm, x, row, tiles), sub(here, behind(here)))
                total = add(total, sub(right, left))
                store(w, x, row, kept(plan, total, row, keep, plane_keep, x))
                here = after
        return 0

    lax.fori_loop(0, count // unroll, body, 0)


def kept(plan, total, row, keep, plane_keep, x):
    mask = plan.row_keep(row)
    if keep is not None:
        mask = keep if mask is None else mask & keep
    if plane_keep is not None:
        inside = plane_keep(x)
        mask = inside if mask is None else mask & inside
    if mask is None:
        return total
    return [jnp.where(mask, value, 0.0) for value in total]


def step_backward(plan, v, w, u, acc, ay, az, c, start, count, unroll, row_tiles, tiles, keep, plane_keep, fresh):
    cx, cy, cz, czm = c

    def body(i, _):
        first = start + i * unroll
        for row in row_tiles:
            here = load(v, first, row, tiles)
            temp = load(u, first, row, tiles)
            diff = sub(here, load(v, first - 1, row, tiles))
            flow = mul(load(cx, first - 1, row, tiles), diff)
            part = mul(diff, sub(temp, load(u, first - 1, row, tiles)))
            for k in range(unroll):
                x = first + k
                after, temp_after = load(v, x + 1, row, tiles), load(u, x + 1, row, tiles)
                diff = sub(after, here)
                out = mul(load(cx, x, row, tiles), diff)
                total = add(here, sub(out, flow))
                flow = out
                term = mul(diff, sub(temp_after, temp))
                both = add(part, term)
                part = term
                store(acc, x, row, both if fresh else add(both, load(acc, x, row, tiles)))
                diff = sub(load(v, x, row + 1, tiles), here)
                up = mul(load(cy, x, row, tiles), diff)
                down = mul(load(cy, x, row - 1, tiles), sub(here, load(v, x, row - 1, tiles)))
                total = add(total, sub(up, down))
                term = mul(diff, sub(load(u, x, row + 1, tiles), temp))
                store(ay, x, row, term if fresh else add(term, load(ay, x, row, tiles)))
                diff = sub(ahead(here), here)
                right = mul(load(cz, x, row, tiles), diff)
                left = mul(load(czm, x, row, tiles), sub(here, behind(here)))
                total = add(total, sub(right, left))
                term = mul(diff, sub(ahead(temp), temp))
                store(az, x, row, term if fresh else add(term, load(az, x, row, tiles)))
                store(w, x, row, kept(plan, total, row, keep, plane_keep, x))
                here, temp = after, temp_after
        return 0

    lax.fori_loop(0, count // unroll, body, 0)


def plane_keeper(plan):
    if not plan.two_sided:
        return None
    low = jnp.where(plan.first("gx"), 1 + HALO, 0)
    high = jnp.where(plan.last("gx"), 1 + HALO + plan.nx, plan.planes)
    return lambda x: (x >= low) & (x < high)


def clear_ends(plan, fields):
    zero = jnp.zeros((ROWS, 128), F32)
    nt = plan.tiles
    for field in fields:
        for t in range(nt):
            field[t] = zero
            field[(plan.planes - 1) * nt + t] = zero


def start_kernel(plan, scale, u0, diffusivity, labels, u, k, px, pya, pyb, *px2):
    nt = plan.tiles
    own = plan.own_plane()
    values = [scale[m] for m in range(MATERIALS)]

    def body(x, _):
        for t in range(nt):
            cols = pl.ds(128 * t, 128)
            u[(own + x) * nt + t, pl.ds(OWN, plan.ny), :] = u0[x, :, cols]
            k[(own + x) * nt + t, pl.ds(OWN, plan.ny), :] = (
                diffusivity[x, :, cols] * factor_of(labels[x, :, cols], values) * HALF_RATE
            )
        return 0

    lax.fori_loop(0, plan.nx, body, 0, unroll=2)
    send_faces(plan, (u, k), px, px2[0] if px2 else None, pya, pyb)


def factor_of(labels, values):
    out = jnp.zeros(labels.shape, F32) + values[0]
    for m in range(1, MATERIALS):
        out = jnp.where(labels == m, values[m], out)
    return out


def ready_kernel(plan, u, k, xa, xb, ya, yb, ca, cb, u_out, k_out, cx, cy, cz, czm, eu, ek, pz):
    del u, k
    place_halos(plan, (u_out, k_out), xa, xb, ya, yb, ca, cb)
    face_coefficients(plan, k_out, cx, cy, cz, czm, plan.planes, plan.tiles)
    pack_edges(plan, u_out, eu, plan.row_tiles)
    pack_edges(plan, k_out, ek, plan.row_tiles)
    pack_faces(plan, eu, pz, 0)
    pack_faces(plan, ek, pz, plan.face_vregs)


def forward_kernel(plan, u0, cx, cy, cz, czm, u1, u2, u3, u4):
    fields = (u0, u1, u2, u3, u4)
    clear_ends(plan, fields[1:ITERS])
    keeper = plane_keeper(plan)
    for n in range(ITERS):
        start, count = plan.span(n)
        tiles = plan.own_tiles if n == ITERS - 1 else plan.row_tiles
        step_forward(plan, fields[n], fields[n + 1], (cx, cy, cz, czm), start, count, plan.unroll, tiles, plan.tiles, None, keeper)


def edge_forward_kernel(plan, eu, ek, za, zb, e0, u1, u2, u3, u4, cx, cy, cz, czm, k):
    e0[...] = eu[...]
    k[...] = ek[...]
    place_faces(plan, e0, za, zb, 0)
    place_faces(plan, k, za, zb, plan.face_vregs)
    wrap_planes(plan, e0)
    wrap_planes(plan, k)
    face_coefficients(plan, k, cx, cy, cz, czm, plan.edge_planes, 1)
    keep = plan.edge_keep()
    keeper = edge_keeper(plan)
    fields = (e0, u1, u2, u3, u4)
    for n in range(ITERS):
        step_forward(plan, fields[n], fields[n + 1], (cx, cy, cz, czm), 1, plan.per_group, edge_unroll(plan), plan.row_tiles, 1, keep, keeper)
        wrap_planes(plan, fields[n + 1])


def edge_unroll(plan):
    return 3 if plan.per_group % 3 == 0 else 2


def edge_keeper(plan):
    group = lanes() // BLOCK
    low = jnp.where(plan.first("gx"), plan.own_plane(), 1)
    high = jnp.where(plan.last("gx"), plan.own_plane() + plan.nx, plan.planes)

    def inside(i):
        plane = group * plan.per_group + i
        return (plane >= low) & (plane < high)

    return inside if plan.two_sided else None


def middle_kernel(plan, u4, e4, measured, observed, adjoint, lam, px, pya, pyb, *px2):
    nt = plan.tiles
    own = plan.own_plane()

    def body(x, _):
        for row in plan.own_tiles:
            temp = merge_edges(plan, load(u4, own + x, row, nt), e4, own + x, row)
            for t in range(nt):
                at = (x, pl.ds(row - OWN, 8), pl.ds(128 * t, 128))
                temp[t] = adjoint[at] + observed[at].astype(F32) * (temp[t] - measured[at])
            store(lam, own + x, row, temp)
        return 0

    lax.fori_loop(0, plan.nx, body, 0, unroll=2)
    send_faces(plan, (lam,), px, px2[0] if px2 else None, pya, pyb)


def turn_kernel(plan, lam, xa, xb, ya, yb, ca, cb, lam_out, edge, pz):
    del lam
    place_halos(plan, (lam_out,), xa, xb, ya, yb, ca, cb)
    pack_edges(plan, lam_out, edge, plan.row_tiles)
    pack_faces(plan, edge, pz, 0)


def backward_kernel(plan, lam, u0, u1, u2, u3, cx, cy, cz, czm, w, other, acc, ay, az):
    fields = (u0, u1, u2, u3)
    clear_ends(plan, (w, other))
    keeper = plane_keeper(plan)
    nt = plan.tiles
    buffers = [lam, other, w, other, w]
    for m in range(ITERS):
        start, count = plan.span(m)
        tiles = plan.own_tiles if m == ITERS - 1 else plan.row_tiles
        n = ITERS - 1 - m
        step_backward(
            plan, buffers[m], buffers[m + 1], fields[n], acc, ay, az, (cx, cy, cz, czm),
            start, count, plan.unroll, tiles, nt, None, keeper, m == 0,
        )
    own = plan.own_plane()

    def body(x, _):
        at, row = own + x, OWN - 8
        v, u = buffers[ITERS - 1], fields[0]
        term = mul(
            sub(load(v, at, row + 1, nt), load(v, at, row, nt)),
            sub(load(u, at, row + 1, nt), load(u, at, row, nt)),
        )
        for t in range(nt):
            ay[at * nt + t, pl.ds(OWN - 1, 1), :] += term[t][7:8]
        return 0

    lax.fori_loop(0, plan.nx, body, 0, unroll=4)


def edge_backward_kernel(plan, lam, za, zb, u0, u1, u2, u3, cx, cy, cz, czm, w, total, e, other, acc, ay, az):
    e[...] = lam[...]
    place_faces(plan, e, za, zb, 0)
    wrap_planes(plan, e)
    keep = plan.edge_keep()
    keeper = edge_keeper(plan)
    fields = (u0, u1, u2, u3)
    buffers = [e, other, w, other, w]
    for m in range(ITERS):
        n = ITERS - 1 - m
        step_backward(
            plan, buffers[m], buffers[m + 1], fields[n], acc, ay, az, (cx, cy, cz, czm),
            1, plan.per_group, edge_unroll(plan), plan.row_tiles, 1, keep, keeper, m == 0,
        )
        if m < ITERS - 1:
            wrap_planes(plan, buffers[m + 1])

    def body(i, _):
        for row in plan.own_tiles:
            z = [az[i + 1, pl.ds(row, 8), :]]
            whole = acc[i + 1, pl.ds(row, 8), :] + ay[i + 1, pl.ds(row, 8), :] + ay[i + 1, pl.ds(row - 1, 8), :]
            total[i + 1, pl.ds(row, 8), :] = whole + z[0] + behind(z)[0]
        return 0

    lax.fori_loop(0, plan.per_group, body, 0)


def finish_kernel(plan, scale, labels, lam, acc, ay, az, e_lam, e_total, gradient, adjoint):
    nt = plan.tiles
    own = plan.own_plane()
    values = [scale[m] for m in range(MATERIALS)]

    def body(x, _):
        p = own + x
        for row in plan.own_tiles:
            z = load(az, p, row, nt)
            total = add(load(acc, p, row, nt), add(load(ay, p, row, nt), load(ay, p, row - 1, nt)))
            total = add(total, add(z, behind(z)))
            total = merge_edges(plan, total, e_total, p, row)
            end = merge_edges(plan, load(lam, p, row, nt), e_lam, p, row)
            for t in range(nt):
                at = (x, pl.ds(row - OWN, 8), pl.ds(128 * t, 128))
                gradient[at] = total[t] * (-HALF_RATE) * factor_of(labels[at], values)
                adjoint[at] = end[t]
        return 0

    lax.fori_loop(0, plan.nx, body, 0, unroll=2)


def call(kernel, plan, outs, args, alias=None, scratch=(), smem=0, flops=0):
    specs = [in_smem] * smem + [in_vmem] * (len(args) - smem)
    cost = pl.CostEstimate(flops=flops, bytes_accessed=flops, transcendentals=0) if flops else None
    return pl.pallas_call(
        functools.partial(kernel, plan),
        out_shape=tuple(outs),
        in_specs=specs,
        out_specs=(in_vmem,) * len(outs),
        input_output_aliases=alias or {},
        scratch_shapes=list(scratch),
        cost_estimate=cost,
        compiler_params=params(),
        name=kernel.__name__,
    )(*args)


def shards(plan, checkpoint, diffusivity, material_scale, labels, measured, observed, adjoint_in):
    nt = plan.tiles
    work = vm(plan.planes * nt, ROWS, 128)
    edge = vm(plan.edge_planes, ROWS, 128)
    wide = HALO * nt

    def faces(count):
        x = vm(count * wide, plan.ny, 128)
        y = vm(plan.nx * nt * count // 2, 2 * HALO, 128)
        return (x, y, y) + ((x,) if plan.two_sided else ())

    def exchange(count, sent):
        px, pya, pyb = sent[:3]
        px2 = sent[3] if plan.two_sided else None
        xa, xb = swap(plan, "gx", px, px2, False)
        ya, yb = swap(plan, "gy", pya, pyb, False)
        per = nt * count // 2
        corner = vm(2 * HALO * per, 2 * HALO, 128)
        body = functools.partial(corner_kernel, plan, per)
        if plan.two_sided:
            shapes, fn = (corner, corner), body
        else:
            shapes, fn = (corner,), lambda ya, yb, out: body(ya, yb, out, None)
        corners = pl.pallas_call(
            fn, out_shape=shapes, in_specs=[in_vmem] * 2, out_specs=(in_vmem,) * len(shapes),
            compiler_params=params(), name="corner_kernel",
        )(ya, yb)
        ca, cb = swap(plan, "gx", corners[0], corners[-1], False)
        return xa, xb, ya, yb, ca, cb

    u, k, *sent = call(start_kernel, plan, (work, work) + faces(2), (material_scale, checkpoint, diffusivity, labels), smem=1)
    got = exchange(2, sent)
    u, k, cx, cy, cz, czm, eu, ek, pz = call(
        ready_kernel, plan, (work, work, work, work, work, work, edge, edge, vm(2 * plan.face_vregs, 8, 128)),
        (u, k) + got, alias={0: 0, 1: 1},
    )
    c = (cx, cy, cz, czm)
    za, zb = swap(plan, "gz", pz, pz, True)
    u1, u2, u3, u4 = call(forward_kernel, plan, (work,) * 4, (u,) + c, flops=1 << 24)
    e0, e1, e2, e3, e4, ex, ey, ez, ezm = call(edge_forward_kernel, plan, (edge,) * 9, (eu, ek, za, zb), scratch=(edge,))
    lam, *sent = call(middle_kernel, plan, (work,) + faces(1), (u4, e4, measured, observed, adjoint_in))
    got = exchange(1, sent)
    lam, e_lam, pz = call(turn_kernel, plan, (work, edge, vm(plan.face_vregs, 8, 128)), (lam,) + got, alias={0: 0})
    za, zb = swap(plan, "gz", pz, pz, True)
    start, _, acc, ay, az = call(backward_kernel, plan, (work,) * 5, (lam, u, u1, u2, u3) + c, flops=1 << 25)
    e_start, e_total = call(
        edge_backward_kernel, plan, (edge,) * 2, (e_lam, za, zb, e0, e1, e2, e3, ex, ey, ez, ezm), scratch=(edge,) * 5
    )
    block = jax.ShapeDtypeStruct((plan.nx, plan.ny, plan.nz), F32)
    return call(finish_kernel, plan, (block, block), (material_scale, labels, start, acc, ay, az, e_start, e_total), smem=1)


def solution(mesh):
    spec = P("gx", "gy", "gz")

    def run(*args):
        plan = Plan(mesh, args[0].shape)
        return jax.shard_map(
            functools.partial(shards, plan),
            mesh=mesh,
            in_specs=(spec, spec, P(), spec, spec, spec, spec),
            out_specs=(spec, spec),
            check_vma=False,
        )(*args)

    return run
```

```python
import functools

import jax
import jax.numpy as jnp
from jax import lax
from jax.experimental import pallas as pl
from jax.experimental.pallas import tpu as pltpu
from jax.sharding import PartitionSpec as P

ITERS = 4
MATERIALS = 4
HALO = ITERS
HALF_RATE = 0.5 * 0.15
OWN = HALO
GROUPS = 4
BLOCK = 128 // GROUPS
F32 = jnp.float32

in_vmem = pl.BlockSpec(memory_space=pltpu.VMEM)
in_smem = pl.BlockSpec(memory_space=pltpu.SMEM)
anywhere = pl.BlockSpec(memory_space=pl.ANY)


def params(mib=3):
    return pltpu.CompilerParams(vmem_limit_bytes=mib << 20)


def vm(*shape):
    return pltpu.VMEM(shape, F32)


def lanes():
    return lax.broadcasted_iota(jnp.int32, (8, 128), 1)


def sublanes():
    return lax.broadcasted_iota(jnp.int32, (8, 128), 0)


def each(fn, *lists):
    return [fn(*items) for items in zip(*lists)]


def add(a, b):
    return each(lambda x, y: x + y, a, b)


def sub(a, b):
    return each(lambda x, y: x - y, a, b)


def mul(a, b):
    return each(lambda x, y: x * y, a, b)


def load(ref, x, row, tiles):
    if row < 0:
        return [pltpu.roll(value, 1, axis=0) for value in load(ref, x, 0, tiles)]
    if row + 8 > ref.shape[1]:
        return [pltpu.roll(value, 7, axis=0) for value in load(ref, x, row - 1, tiles)]
    return [ref[x * tiles + t, pl.ds(row, 8), :] for t in range(tiles)]


def store(ref, x, row, values):
    for t, value in enumerate(values):
        ref[x * len(values) + t, pl.ds(row, 8), :] = value


def ahead(values):
    rolled = [pltpu.roll(v, 127, axis=1) for v in values]
    count = len(values)
    if count == 1:
        return rolled
    last = lanes() == 127
    return [jnp.where(last, rolled[(t + 1) % count], rolled[t]) for t in range(count)]


def behind(values):
    rolled = [pltpu.roll(v, 1, axis=1) for v in values]
    count = len(values)
    if count == 1:
        return rolled
    first = lanes() == 0
    return [jnp.where(first, rolled[(t - 1) % count], rolled[t]) for t in range(count)]


class Plan:
    def __init__(self, mesh, shape):
        self.sizes = {axis: mesh.shape[axis] for axis in ("gx", "gy", "gz")}
        self.nx = shape[0] // self.sizes["gx"]
        self.ny = shape[1] // self.sizes["gy"]
        self.nz = shape[2] // self.sizes["gz"]
        self.tiles = self.nz // 128
        self.rows = self.ny + 2 * HALO
        self.two_sided = self.sizes["gx"] > 2
        self.deep = self.nx + HALO * (2 if self.two_sided else 1)
        self.planes = self.deep + 2
        self.per_group = self.deep // GROUPS
        self.edge_planes = self.per_group + 2
        self.row_tiles = [OWN - HALO + 8 * t for t in range((self.ny + 2 * HALO) // 8)]
        self.own_tiles = [OWN + 8 * t for t in range(self.ny // 8)]
        self.end_tiles = [self.row_tiles[0], self.row_tiles[-1]]
        self.edge_vregs = self.per_group * len(self.row_tiles)
        self.face_vregs = -(-self.edge_vregs // 4)

    def index(self, axis):
        return lax.axis_index(axis)

    def even(self, axis):
        return lax.rem(lax.axis_index(axis), 2) == 0

    def first(self, axis):
        return lax.axis_index(axis) == 0

    def last(self, axis):
        return lax.axis_index(axis) == self.sizes[axis] - 1

    def own_plane(self):
        if self.two_sided:
            return jnp.int32(1 + HALO)
        return jnp.where(self.even("gx"), 1, 1 + HALO)

    def core(self):
        own = self.own_plane()
        if self.two_sided:
            return own + HALO, self.nx - 2 * HALO
        return own + jnp.where(self.even("gx"), 0, HALO), self.nx - HALO

    def beside(self, low, high, count):
        own = self.own_plane()
        if self.two_sided:
            return [(own + low, count), (own + high, count)]
        return [(own + jnp.where(self.even("gx"), high, low), count)]

    def strips(self, step):
        count = HALO - 1 - step
        return self.beside(step + 1, self.nx - HALO, count) if count else []

    def rims(self, step):
        return self.beside(step + 1 - HALO, self.nx - HALO, 2 * HALO - 1 - step)

    def masks(self):
        return {row: self.row_keep(row) for row in self.row_tiles + self.own_tiles}

    def row_keep(self, row):
        if row < OWN:
            return (sublanes() >= OWN - row) | jnp.logical_not(self.first("gy"))
        if row + 8 > OWN + self.ny:
            return (sublanes() < OWN + self.ny - row) | jnp.logical_not(self.last("gy"))
        return None

    def edge_keep(self):
        pos = lanes() % BLOCK
        low = (pos >= 16) & (pos < 20) & self.first("gz")
        high = (pos >= 12) & (pos < 16) & self.last("gz")
        return jnp.logical_not(low | high)


def pairs(count, second):
    if not second:
        return [(i, i ^ 1) for i in range(count)]
    inner = [(i, i + 1) for i in range(1, count - 1, 2)]
    return inner + [(b, a) for a, b in inner]


def swap(plan, axis, first, second, wrap):
    count = plan.sizes[axis]
    got = lax.ppermute(first, axis, pairs(count, False))
    if count == 2:
        return got, got
    ends = [(0, count - 1), (count - 1, 0)] if wrap else [(0, 0), (count - 1, count - 1)]
    return got, lax.ppermute(second, axis, pairs(count, True) + ends)


def send_faces(plan, fields, px, px2, pya, pyb):
    nt = plan.tiles
    own = plan.own_plane()
    even_x, even_y = plan.even("gx"), plan.even("gy")
    wide = HALO * nt
    rows = pl.ds(OWN, plan.ny)
    low, high = own * nt, (own + plan.nx - HALO) * nt
    for f, field in enumerate(fields):
        at = jnp.where(even_x, high, low)
        for j in range(wide):
            px[f * wide + j] = field[at + j, rows, :]
        if plan.two_sided:
            at = jnp.where(even_x, low, high)
            for j in range(wide):
                px2[f * wide + j] = field[at + j, rows, :]
    top = OWN + plan.ny - HALO

    def body(x, _):
        for f, field in enumerate(fields):
            for t in range(nt):
                a = field[(own + x) * nt + t, pl.ds(OWN, HALO), :]
                b = field[(own + x) * nt + t, pl.ds(top, HALO), :]
                if len(fields) == 2:
                    to = (x * nt + t, pl.ds(HALO * f, HALO))
                else:
                    to = (x * (nt // 2) + t // 2, pl.ds(HALO * (t % 2), HALO))
                pya[to[0], to[1], :] = jnp.where(even_y, b, a)
                pyb[to[0], to[1], :] = jnp.where(even_y, a, b)
        return 0

    lax.fori_loop(0, plan.nx, body, 0, unroll=4)


def corners(plan, per, ya, yb, out, out2=None):
    even = plan.even("gx")
    low, high = 0, (plan.nx - HALO) * per
    width = HALO * per
    at = jnp.where(even, high, low)
    for n, ref in enumerate((ya, yb)):
        out[n * width : (n + 1) * width] = ref[pl.ds(at, width)]
    if plan.two_sided:
        at = jnp.where(even, low, high)
        for n, ref in enumerate((ya, yb)):
            out2[n * width : (n + 1) * width] = ref[pl.ds(at, width)]


def place_halos(plan, fields, xa, xb, ya, yb, ca, cb):
    nt = plan.tiles
    own = plan.own_plane()
    wide = HALO * nt
    even_x, even_y = plan.even("gx"), plan.even("gy")
    two = len(fields) == 2
    per = nt if two else nt // 2
    below, above = own - HALO, own + plan.nx
    rows = pl.ds(OWN, plan.ny)

    def put_rows(plane, source_a, source_b, at, blank):
        for f, field in enumerate(fields):
            for t in range(nt):
                if two:
                    a = source_a[at + t, pl.ds(HALO * f, HALO), :]
                    b = source_b[at + t, pl.ds(HALO * f, HALO), :]
                else:
                    a = source_a[at + t // 2, pl.ds(HALO * (t % 2), HALO), :]
                    b = source_b[at + t // 2, pl.ds(HALO * (t % 2), HALO), :]
                low = jnp.where(even_y, b, a)
                high = jnp.where(even_y, a, b)
                low = jnp.where(plan.first("gy") | blank, 0.0, low)
                high = jnp.where(plan.last("gy") | blank, 0.0, high)
                field[plane * nt + t, pl.ds(OWN - HALO, HALO), :] = low
                field[plane * nt + t, pl.ds(OWN + plan.ny, HALO), :] = high

    def body(x, _):
        put_rows(own + x, ya, yb, x * per, False)
        return 0

    lax.fori_loop(0, plan.nx, body, 0, unroll=4)

    sides = [(xa, ca, jnp.where(even_x, above, below), False)]
    if plan.two_sided:
        sides[0] = (xa, ca, jnp.where(even_x, above, below), False)
        ends = (even_x & plan.first("gx")) | (jnp.logical_not(even_x) & plan.last("gx"))
        sides.append((xb, cb, jnp.where(even_x, below, above), ends))
    for x_ref, c_ref, plane, blank in sides:
        for f, field in enumerate(fields):
            for j in range(wide):
                value = x_ref[f * wide + j]
                if blank is not False:
                    value = jnp.where(blank, 0.0, value)
                field[plane * nt + j, rows, :] = value
        half = HALO * per
        for j in range(HALO):
            put_rows(plane + j, c_ref.at[pl.ds(0, half)], c_ref.at[pl.ds(half, half)], j * per, blank)
    zero = jnp.zeros((plan.rows, 128), F32)
    for field in fields:
        for t in range(nt):
            field[t] = zero
            field[(plan.planes - 1) * nt + t] = zero


def pack_edges(plan, field, edge, row_tiles):
    nt = plan.tiles
    masks = [lanes() >= 16 * j for j in range(2 * GROUPS)]

    def body(i, _):
        for row in row_tiles:
            value = None
            for g in range(GROUPS):
                plane = (g * plan.per_group + 1 + i) * nt
                right = pltpu.roll(field[plane + nt - 1, pl.ds(row, 8), :], (BLOCK * g + 12) % 128, axis=1)
                left = pltpu.roll(field[plane, pl.ds(row, 8), :], (BLOCK * g + 20) % 128, axis=1)
                value = right if value is None else jnp.where(masks[2 * g], right, value)
                value = jnp.where(masks[2 * g + 1], left, value)
            edge[i + 1, pl.ds(row, 8), :] = value
        return 0

    lax.fori_loop(0, plan.per_group, body, 0)


def edge_places(plan):
    return [(i + 1, row) for i in range(plan.per_group) for row in plan.row_tiles]


def pack_faces(plan, edge, out, base):
    lane = lanes()
    places = edge_places(plan)
    for q in range(plan.face_vregs):
        value = None
        for slot, (i, row) in enumerate(places[4 * q : 4 * q + 4]):
            held = edge[i, pl.ds(row, 8), :]
            low = pltpu.roll(held, (8 * slot - 20) % 128, axis=1)
            high = pltpu.roll(held, (8 * slot - 4) % 128, axis=1)
            both = jnp.where(lane % 8 < 4, low, high)
            value = both if value is None else jnp.where(lane % BLOCK >= 8 * slot, both, value)
        out[base + q] = value


def place_faces(plan, edge, za, zb, base):
    lane = lanes()
    pos = lane % BLOCK
    halo = (pos >= 12) & (pos < 20)
    even = plan.even("gz")
    places = edge_places(plan)
    for q in range(plan.face_vregs):
        a, b = za[base + q], zb[base + q]
        right = jnp.where(plan.last("gz"), 0.0, jnp.where(even, a, b))
        left = jnp.where(plan.first("gz"), 0.0, jnp.where(even, b, a))
        both = jnp.where(lane % 8 < 4, right, left)
        for slot, (i, row) in enumerate(places[4 * q : 4 * q + 4]):
            moved = pltpu.roll(both, (12 - 8 * slot) % 128, axis=1)
            edge[i, pl.ds(row, 8), :] = jnp.where(halo, moved, edge[i, pl.ds(row, 8), :])


def wrap_planes(plan, edge):
    lane = lanes()
    last = plan.per_group
    for row in plan.row_tiles:
        before = pltpu.roll(edge[last, pl.ds(row, 8), :], BLOCK, axis=1)
        after = pltpu.roll(edge[1, pl.ds(row, 8), :], 128 - BLOCK, axis=1)
        edge[0, pl.ds(row, 8), :] = jnp.where(lane < BLOCK, 0.0, before)
        edge[last + 1, pl.ds(row, 8), :] = jnp.where(lane >= 128 - BLOCK, 0.0, after)


def merge_edges(plan, values, edge, plane, row):
    lane = lanes()
    g = (plane - 1) // plan.per_group
    i = plane - g * plan.per_group
    held = edge[i, pl.ds(row, 8), :]
    left = pltpu.roll(held, lax.rem(256 - 20 - BLOCK * g, 128), axis=1)
    right = pltpu.roll(held, lax.rem(256 - 12 - BLOCK * g, 128), axis=1)
    values = list(values)
    values[0] = jnp.where(lane < 4, left, values[0])
    values[-1] = jnp.where(lane >= 124, right, values[-1])
    return values


def face_coefficients(k, c, start, count, rows, tiles, unroll):
    cx, cy, cz, czm = c

    def body(i, _):
        for j in range(unroll):
            x = start + i * unroll + j
            for row in rows:
                here = load(k, x, row, tiles)
                store(cx, x, row, add(here, load(k, x + 1, row, tiles)))
                store(cy, x, row, add(here, load(k, x, row + 1, tiles)))
                store(cz, x, row, add(here, ahead(here)))
                store(czm, x, row, add(here, behind(here)))
        return 0

    repeat(body, count // unroll)


def repeat(body, count):
    if count == 1:
        body(0, 0)
    else:
        lax.fori_loop(0, count, body, 0)


def kept(total, mask, plane_keep, x):
    if plane_keep is not None:
        inside = plane_keep(x)
        mask = inside if mask is None else mask & inside
    if mask is None:
        return total
    return [jnp.where(mask, value, 0.0) for value in total]


def step_forward(v, w, c, start, count, rows, tiles, masks, plane_keep, unroll):
    cx, cy, cz, czm = c

    def body(i, _):
        first = start + i * unroll
        for row in rows:
            here = load(v, first, row, tiles)
            flow = mul(load(cx, first - 1, row, tiles), sub(here, load(v, first - 1, row, tiles)))
            for k in range(unroll):
                x = first + k
                after = load(v, x + 1, row, tiles)
                out = mul(load(cx, x, row, tiles), sub(after, here))
                total = add(here, sub(out, flow))
                flow = out
                up = mul(load(cy, x, row, tiles), sub(load(v, x, row + 1, tiles), here))
                down = mul(load(cy, x, row - 1, tiles), sub(here, load(v, x, row - 1, tiles)))
                total = add(total, sub(up, down))
                right = mul(load(cz, x, row, tiles), sub(ahead(here), here))
                left = mul(load(czm, x, row, tiles), sub(here, behind(here)))
                total = add(total, sub(right, left))
                store(w, x, row, kept(total, masks[row], plane_keep, x))
                here = after
        return 0

    repeat(body, count // unroll)


def step_backward(v, w, u, sums, c, start, count, rows, tiles, masks, plane_keep, unroll, fresh):
    cx, cy, cz, czm = c
    acc, az = sums

    def body(i, _):
        first = start + i * unroll
        for row in rows:
            here = load(v, first, row, tiles)
            temp = load(u, first, row, tiles)
            diff = sub(here, load(v, first - 1, row, tiles))
            flow = mul(load(cx, first - 1, row, tiles), diff)
            part = mul(diff, sub(temp, load(u, first - 1, row, tiles)))
            for k in range(unroll):
                x = first + k
                after, temp_after = load(v, x + 1, row, tiles), load(u, x + 1, row, tiles)
                diff = sub(after, here)
                out = mul(load(cx, x, row, tiles), diff)
                total = add(here, sub(out, flow))
                flow = out
                term = mul(diff, sub(temp_after, temp))
                both = add(part, term)
                part = term
                diff = sub(load(v, x, row + 1, tiles), here)
                less = sub(here, load(v, x, row - 1, tiles))
                up = mul(load(cy, x, row, tiles), diff)
                down = mul(load(cy, x, row - 1, tiles), less)
                total = add(total, sub(up, down))
                both = add(both, mul(diff, sub(load(u, x, row + 1, tiles), temp)))
                both = add(both, mul(less, sub(temp, load(u, x, row - 1, tiles))))
                store(acc, x, row, both if fresh else add(both, load(acc, x, row, tiles)))
                diff = sub(ahead(here), here)
                right = mul(load(cz, x, row, tiles), diff)
                left = mul(load(czm, x, row, tiles), sub(here, behind(here)))
                total = add(total, sub(right, left))
                term = mul(diff, sub(ahead(temp), temp))
                store(az, x, row, term if fresh else add(term, load(az, x, row, tiles)))
                store(w, x, row, kept(total, masks[row], plane_keep, x))
                here, temp = after, temp_after
        return 0

    repeat(body, count // unroll)


def inner_unroll(count):
    return next(n for n in (7, 6, 4, 2, 1) if count % n == 0)


def plane_keeper(plan):
    if not plan.two_sided:
        return None
    low = jnp.where(plan.first("gx"), 1 + HALO, 0)
    high = jnp.where(plan.last("gx"), 1 + HALO + plan.nx, plan.planes)
    return lambda x: (x >= low) & (x < high)


def clear_ends(plan, fields):
    zero = jnp.zeros((plan.rows, 128), F32)
    nt = plan.tiles
    for field in fields:
        for t in range(nt):
            field[t] = zero
            field[(plan.planes - 1) * nt + t] = zero


def factor_of(labels, values):
    out = jnp.zeros(labels.shape, F32) + values[0]
    for m in range(1, MATERIALS):
        out = jnp.where(labels == m, values[m], out)
    return out


def face_kernel(plan, scale, u0, diffusivity, labels, px, pya, pyb, *rest):
    *px2, scale_s, ux, dx, lx, uy, dy, ly, sems = rest
    nt, ny = plan.tiles, plan.ny
    even_x, even_y = plan.even("gx"), plan.even("gy")
    low, high = 0, plan.nx - HALO
    starts = [jnp.where(even_x, high, low)] + ([jnp.where(even_x, low, high)] if plan.two_sided else [])
    copies = [pltpu.make_async_copy(scale, scale_s, sems.at[0])]
    for s, at in enumerate(starts):
        for n, (source, held) in enumerate(((u0, ux), (diffusivity, dx), (labels, lx))):
            copies.append(pltpu.make_async_copy(source.at[pl.ds(at, HALO)], held.at[s], sems.at[1 + 3 * s + n]))
    for s, at in enumerate((0, ny - 8)):
        for n, (source, held) in enumerate(((u0, uy), (diffusivity, dy), (labels, ly))):
            copies.append(
                pltpu.make_async_copy(source.at[:, pl.ds(at, 8), :], held.at[s], sems.at[7 + 3 * s + n])
            )
    for copy in copies:
        copy.start()
    for copy in copies:
        copy.wait()
    values = [scale_s[m] for m in range(MATERIALS)]
    wide = HALO * nt
    for s, out in enumerate((px, *px2)):
        for j in range(HALO):
            for t in range(nt):
                cols = pl.ds(128 * t, 128)
                out[j * nt + t] = ux[s, j, :, cols]
                out[wide + j * nt + t] = dx[s, j, :, cols] * factor_of(lx[s, j, :, cols], values) * HALF_RATE

    def body(x, _):
        for t in range(nt):
            cols = pl.ds(128 * t, 128)
            k = [dy[s, x, :, cols] * factor_of(ly[s, x, :, cols], values) * HALF_RATE for s in range(2)]
            u = [uy[s, x, :, cols] for s in range(2)]
            for f, (a, b) in enumerate((u, k)):
                a, b = a[:HALO], b[8 - HALO :]
                pya[x * nt + t, pl.ds(HALO * f, HALO), :] = jnp.where(even_y, b, a)
                pyb[x * nt + t, pl.ds(HALO * f, HALO), :] = jnp.where(even_y, a, b)
        return 0

    lax.fori_loop(0, plan.nx, body, 0, unroll=4)


def own_kernel(plan, scale, u0, diffusivity, labels, u, k, cx, cy, cz, czm):
    nt = plan.tiles
    own = plan.own_plane()
    values = [scale[m] for m in range(MATERIALS)]
    clear_ends(plan, (u, k))

    def body(x, _):
        for t in range(nt):
            cols = pl.ds(128 * t, 128)
            u[(own + x) * nt + t, pl.ds(OWN, plan.ny), :] = u0[x, :, cols]
            k[(own + x) * nt + t, pl.ds(OWN, plan.ny), :] = (
                diffusivity[x, :, cols] * factor_of(labels[x, :, cols], values) * HALF_RATE
            )
        return 0

    lax.fori_loop(0, plan.nx, body, 0, unroll=2)
    face_coefficients(k, (cx, cy, cz, czm), own - 1, plan.nx + 1, plan.own_tiles, nt, 3)


def inner_forward_kernel(plan, steps, sources, *refs):
    c, fields = refs[:4], refs[4:]
    clear_ends(plan, fields[sources:])
    masks = dict.fromkeys(plan.own_tiles)
    start, count = plan.core()
    for n, step in enumerate(steps):
        v, w = fields[sources - 1 + n], fields[sources + n]
        step_forward(v, w, c, start, count, plan.own_tiles, plan.tiles, masks, None, inner_unroll(count))
        for at, many in plan.strips(step):
            step_forward(v, w, c, at, many, plan.own_tiles, plan.tiles, masks, None, many)


def ready_kernel(plan, xa, xb, ya, yb, ca, cb, u_in, k_in, u, k, eu, ek, pz):
    del u_in, k_in
    place_halos(plan, (u, k), xa, xb, ya, yb, ca, cb)
    pack_edges(plan, u, eu, plan.row_tiles)
    pack_edges(plan, k, ek, plan.row_tiles)
    pack_faces(plan, eu, pz, 0)
    pack_faces(plan, ek, pz, plan.face_vregs)


def outer_forward_kernel(plan, u, k, *refs):
    c, later = refs[8:12], refs[12:]
    nt = plan.tiles
    own = plan.own_plane()
    face_coefficients(k, c, own - 1, plan.nx + 1, plan.end_tiles, nt, 11)
    for at, many in plan.beside(-HALO - 1, plan.nx - HALO - 1, 2 * HALO + 1):
        face_coefficients(k, c, at, many, plan.row_tiles, nt, 3)
    fields = (u, *later)
    masks, keeper = plan.masks(), plane_keeper(plan)
    start, count = plan.core()
    for n in range(ITERS):
        step_forward(fields[n], fields[n + 1], c, start, count, plan.end_tiles, nt, masks, None, 2 * inner_unroll(count))
        for at, many in plan.rims(n):
            step_forward(fields[n], fields[n + 1], c, at, many, plan.row_tiles, nt, masks, keeper, many)


def edge_masks(plan):
    keep = plan.edge_keep()
    return {row: keep if mask is None else keep & mask for row, mask in plan.masks().items()}


def edge_forward_kernel(plan, eu, k_in, za, zb, e0, k, u1, u2, u3, u4, cx, cy, cz, czm):
    del eu, k_in
    place_faces(plan, e0, za, zb, 0)
    place_faces(plan, k, za, zb, plan.face_vregs)
    wrap_planes(plan, e0)
    wrap_planes(plan, k)
    c = (cx, cy, cz, czm)
    face_coefficients(k, c, 0, plan.per_group + 1, plan.row_tiles, 1, plan.per_group + 1)
    masks, keeper = edge_masks(plan), edge_keeper(plan)
    fields = (e0, u1, u2, u3, u4)
    for n in range(ITERS):
        step_forward(fields[n], fields[n + 1], c, 1, plan.per_group, plan.row_tiles, 1, masks, keeper, plan.per_group)
        wrap_planes(plan, fields[n + 1])


def edge_keeper(plan):
    if not plan.two_sided:
        return None
    group = lanes() // BLOCK
    low = jnp.where(plan.first("gx"), plan.own_plane(), 1)
    high = jnp.where(plan.last("gx"), plan.own_plane() + plan.nx, plan.planes)

    def inside(i):
        plane = group * plan.per_group + i
        return (plane >= low) & (plane < high)

    return inside


def middle_kernel(plan, u4, e4, measured, observed, adjoint, lam, px, pya, pyb, *px2):
    nt = plan.tiles
    own = plan.own_plane()

    def body(x, _):
        for row in plan.own_tiles:
            temp = merge_edges(plan, load(u4, own + x, row, nt), e4, own + x, row)
            for t in range(nt):
                at = (x, pl.ds(row - OWN, 8), pl.ds(128 * t, 128))
                temp[t] = adjoint[at] + observed[at].astype(F32) * (temp[t] - measured[at])
            store(lam, own + x, row, temp)
        return 0

    lax.fori_loop(0, plan.nx, body, 0, unroll=4)
    clear_ends(plan, (lam,))
    send_faces(plan, (lam,), px, px2[0] if px2 else None, pya, pyb)


def inner_backward_kernel(plan, steps, fresh, given, *refs):
    c, temps = refs[:4], refs[4 : 4 + len(steps)]
    rest = refs[4 + len(steps) + given :]
    lams, sums = refs[4 + len(steps) : 5 + len(steps)] + rest[: len(steps)], rest[len(steps) :]
    clear_ends(plan, lams[1:])
    masks = dict.fromkeys(plan.own_tiles)
    start, count = plan.core()
    for n, step in enumerate(steps):
        v, w = lams[n], lams[n + 1]
        step_backward(
            v, w, temps[n], sums, c, start, count, plan.own_tiles, plan.tiles, masks, None,
            inner_unroll(count), fresh and n == 0,
        )
        for at, many in plan.strips(step):
            step_forward(v, w, c, at, many, plan.own_tiles, plan.tiles, masks, None, many)


def turn_kernel(plan, xa, xb, ya, yb, ca, cb, lam_in, lam, edge, pz):
    del lam_in
    place_halos(plan, (lam,), xa, xb, ya, yb, ca, cb)
    pack_edges(plan, lam, edge, plan.row_tiles)
    pack_faces(plan, edge, pz, 0)


def outer_backward_kernel(plan, lam, *refs):
    c, temps, rest = refs[:4], refs[4:8], refs[14:]
    later, sums = rest[:4], rest[4:]
    nt = plan.tiles
    fields = (lam, *later)
    masks, keeper = plan.masks(), plane_keeper(plan)
    start, count = plan.core()
    for m in range(ITERS):
        v, w, u = fields[m], fields[m + 1], temps[ITERS - 1 - m]
        step_backward(
            v, w, u, sums, c, start, count, plan.end_tiles, nt, masks, None, 2 * inner_unroll(count), m == 0
        )
        for at, many in plan.rims(m):
            step_backward(v, w, u, sums, c, at, many, plan.row_tiles, nt, masks, keeper, many, m == 0)


def edge_backward_kernel(plan, lam, za, zb, u0, u1, u2, u3, cx, cy, cz, czm, w, total, e, other, acc, az):
    e[...] = lam[...]
    place_faces(plan, e, za, zb, 0)
    wrap_planes(plan, e)
    masks, keeper = edge_masks(plan), edge_keeper(plan)
    fields = (u0, u1, u2, u3)
    buffers = [e, other, w, other, w]
    for m in range(ITERS):
        n = ITERS - 1 - m
        step_backward(
            buffers[m], buffers[m + 1], fields[n], (acc, az), (cx, cy, cz, czm),
            1, plan.per_group, plan.row_tiles, 1, masks, keeper, plan.per_group, m == 0,
        )
        if m < ITERS - 1:
            wrap_planes(plan, buffers[m + 1])
    for i in range(1, 1 + plan.per_group):
        for row in plan.own_tiles:
            z = [az[i, pl.ds(row, 8), :]]
            total[i, pl.ds(row, 8), :] = acc[i, pl.ds(row, 8), :] + z[0] + behind(z)[0]


def finish_kernel(plan, scale, labels, lam, acc, az, e_lam, e_total, gradient, adjoint, grad_s, adj_s, sems):
    nt = plan.tiles
    own = plan.own_plane()
    values = [scale[m] for m in range(MATERIALS)]
    chunk = 4

    def copies(i):
        at = pl.ds(i * chunk, chunk)
        return (
            pltpu.make_async_copy(grad_s.at[at], gradient.at[at], sems.at[0, i]),
            pltpu.make_async_copy(adj_s.at[at], adjoint.at[at], sems.at[1, i]),
        )

    def body(i, _):
        for j in range(chunk):
            x = i * chunk + j
            p = own + x
            for row in plan.own_tiles:
                z = load(az, p, row, nt)
                total = add(load(acc, p, row, nt), add(z, behind(z)))
                total = merge_edges(plan, total, e_total, p, row)
                end = merge_edges(plan, load(lam, p, row, nt), e_lam, p, row)
                for t in range(nt):
                    at = (x, pl.ds(row - OWN, 8), pl.ds(128 * t, 128))
                    grad_s[at] = total[t] * (-HALF_RATE) * factor_of(labels[at], values)
                    adj_s[at] = end[t]
        for copy in copies(i):
            copy.start()
        return 0

    lax.fori_loop(0, plan.nx // chunk, body, 0)

    def drain(i, _):
        for copy in copies(i):
            copy.wait()
        return 0

    lax.fori_loop(0, plan.nx // chunk, drain, 0)


def call(kernel, outs, args, alias=None, scratch=(), smem=0, flops=0, specs=None, out_spec=in_vmem, mib=3):
    if specs is None:
        specs = [in_smem] * smem + [in_vmem] * (len(args) - smem)
    cost = pl.CostEstimate(flops=flops, bytes_accessed=flops, transcendentals=0) if flops else None
    return pl.pallas_call(
        kernel,
        out_shape=tuple(outs),
        in_specs=specs,
        out_specs=(out_spec,) * len(outs),
        input_output_aliases=alias or {},
        scratch_shapes=list(scratch),
        cost_estimate=cost,
        compiler_params=params(mib),
        name=kernel.func.__name__,
    )(*args)


def shards(plan, checkpoint, diffusivity, material_scale, labels, measured, observed, adjoint_in):
    nt, nx, ny, nz = plan.tiles, plan.nx, plan.ny, plan.nz
    part = functools.partial
    work = vm(plan.planes * nt, plan.rows, 128)
    edge = vm(plan.edge_planes, plan.rows, 128)
    sides = 2 if plan.two_sided else 1

    def faces(count):
        x = vm(count * HALO * nt, ny, 128)
        y = vm(nx * nt * count // 2, 2 * HALO, 128)
        return (x, y, y) + (x,) * (sides - 1)

    def exchange(count, sent, between):
        px, pya, pyb = sent[:3]
        xa, xb = swap(plan, "gx", px, sent[-1], False)
        ya, yb = swap(plan, "gy", pya, pyb, False)
        per = nt * count // 2
        corner = vm(2 * HALO * per, 2 * HALO, 128)

        def corner_kernel(ya, yb, _, *out):
            corners(plan, per, ya, yb, *out)

        got = call(part(corner_kernel), (corner,) * sides, (ya, yb, between()))
        ca, cb = swap(plan, "gx", got[0], got[-1], False)
        return (xa, xb, ya, yb, ca, cb), got[0]

    hbm = [pltpu.with_memory_space_constraint(a, pltpu.HBM) for a in (material_scale, checkpoint, diffusivity, labels)]
    held = [vm(sides, HALO, ny, nz)] * 2 + [pltpu.VMEM((sides, HALO, ny, nz), jnp.int32)]
    held += [vm(2, nx, 8, nz)] * 2 + [pltpu.VMEM((2, nx, 8, nz), jnp.int32)]
    sent = call(
        part(face_kernel, plan), faces(2), hbm, specs=[anywhere] * 4, mib=8,
        scratch=[pltpu.SMEM((MATERIALS,), F32), *held, pltpu.SemaphoreType.DMA((13,))],
    )
    u, k, *c = call(part(own_kernel, plan), (work,) * 6, (material_scale, checkpoint, diffusivity, labels), smem=1, flops=1 << 23)
    state = {}

    def first_half():
        state["c"], state["u"], state["new"] = c, u, call(
            part(lambda *refs: inner_forward_kernel(plan, (0, 1), 1, *refs)), (work,) * 2, (*c, u), flops=1 << 23
        )
        return state["new"][0]

    got, mark = exchange(2, sent, first_half)
    u1, u2 = state["new"]

    def later_half(mark, *refs):
        del mark
        inner_forward_kernel(plan, (2, 3), 1, *refs)

    u3, u4 = call(part(later_half), (work,) * 2, (mark, *c, u2), flops=1 << 23)
    u, k, eu, ek, pz = call(
        part(after(ready_kernel), plan), (work, work, edge, edge, vm(2 * plan.face_vregs, 8, 128)),
        (u4, *got, u, k), alias={7: 0, 8: 1},
    )
    za, zb = swap(plan, "gz", pz, pz, True)
    out = call(
        part(outer_forward_kernel, plan), (work,) * 8, (u, k, *c, u1, u2, u3, u4),
        alias={2 + i: i for i in range(8)}, flops=1 << 24,
    )
    c, (u1, u2, u3, u4) = out[:4], out[4:]
    e0, _, e1, e2, e3, e4, ex, ey, ez, ezm = call(
        part(edge_forward_kernel, plan), (edge,) * 10, (eu, ek, za, zb), alias={0: 0, 1: 1}
    )
    lam, *sent = call(
        part(middle_kernel, plan), (work,) + faces(1), (u4, e4, measured, observed, adjoint_in), alias={0: 0}
    )

    def first_back():
        state["new"] = call(
            part(lambda *refs: inner_backward_kernel(plan, (0, 1), True, 1, *refs)), (work,) * 4,
            (*c, u3, u2, lam), flops=1 << 24,
        )
        return state["new"][0]

    got, mark = exchange(1, sent, first_back)
    l3, l2, acc, az = state["new"]

    def later_back(mark, *refs):
        del mark
        inner_backward_kernel(plan, (2, 3), False, 3, *refs)

    l1, l0, acc, az = call(
        part(later_back), (work,) * 4, (mark, *c, u1, u, l2, acc, az), alias={8: 2, 9: 3}, flops=1 << 24
    )
    lam, e_lam, pz = call(
        part(after(turn_kernel), plan), (work, edge, vm(plan.face_vregs, 8, 128)), (l0, *got, lam), alias={7: 0}
    )
    za, zb = swap(plan, "gz", pz, pz, True)
    l3, l2, l1, l0, acc, az = call(
        part(outer_backward_kernel, plan), (work,) * 6, (lam, *c, u, u1, u2, u3, l3, l2, l1, l0, acc, az),
        alias={9 + i: i for i in range(6)}, flops=1 << 25,
    )
    e_start, e_total = call(
        part(edge_backward_kernel, plan), (edge,) * 2, (e_lam, za, zb, e0, e1, e2, e3, ex, ey, ez, ezm), scratch=(edge,) * 4
    )
    block = jax.ShapeDtypeStruct((nx, ny, nz), F32)
    return call(
        part(finish_kernel, plan), (block, block), (material_scale, labels, l0, acc, az, e_start, e_total), smem=1,
        out_spec=anywhere, mib=6, scratch=[vm(nx, ny, nz), vm(nx, ny, nz), pltpu.SemaphoreType.DMA((2, nx // 4))],
    )


def after(kernel):
    @functools.wraps(kernel)
    def waiting(plan, _, *refs):
        kernel(plan, *refs)

    return waiting


def solution(mesh):
    spec = P("gx", "gy", "gz")

    def run(*args):
        plan = Plan(mesh, args[0].shape)
        return jax.shard_map(
            functools.partial(shards, plan),
            mesh=mesh,
            in_specs=(spec, spec, P(), spec, spec, spec, spec),
            out_specs=(spec, spec),
            check_vma=False,
        )(*args)

    return run
```

```python
import functools

import jax
import jax.numpy as jnp
from jax import lax
from jax.experimental import pallas as pl
from jax.experimental.pallas import tpu as pltpu
from jax.sharding import PartitionSpec as P

ITERS = 4
MATERIALS = 4
HALO = ITERS
HALF_RATE = 0.5 * 0.15
OWN = HALO
GROUPS = 4
BLOCK = 128 // GROUPS
F32 = jnp.float32

in_vmem = pl.BlockSpec(memory_space=pltpu.VMEM)
in_smem = pl.BlockSpec(memory_space=pltpu.SMEM)
anywhere = pl.BlockSpec(memory_space=pl.ANY)


def params(mib=3):
    return pltpu.CompilerParams(vmem_limit_bytes=mib << 20)


def vm(*shape):
    return pltpu.VMEM(shape, F32)


def lanes():
    return lax.broadcasted_iota(jnp.int32, (8, 128), 1)


def sublanes():
    return lax.broadcasted_iota(jnp.int32, (8, 128), 0)


def each(fn, *lists):
    return [fn(*items) for items in zip(*lists)]


def add(a, b):
    return each(lambda x, y: x + y, a, b)


def sub(a, b):
    return each(lambda x, y: x - y, a, b)


def mul(a, b):
    return each(lambda x, y: x * y, a, b)


def load(ref, x, row, tiles):
    if row < 0:
        return [pltpu.roll(value, 1, axis=0) for value in load(ref, x, 0, tiles)]
    if row + 8 > ref.shape[1]:
        return [pltpu.roll(value, 7, axis=0) for value in load(ref, x, row - 1, tiles)]
    return [ref[x * tiles + t, pl.ds(row, 8), :] for t in range(tiles)]


def store(ref, x, row, values):
    for t, value in enumerate(values):
        ref[x * len(values) + t, pl.ds(row, 8), :] = value


def ahead(values):
    rolled = [pltpu.roll(v, 127, axis=1) for v in values]
    last = lanes() == 127
    return [jnp.where(last, b, a) for a, b in zip(rolled, rolled[1:])] + rolled[-1:]


def behind(values):
    rolled = [pltpu.roll(v, 1, axis=1) for v in values]
    first = lanes() == 0
    return rolled[:1] + [jnp.where(first, a, b) for a, b in zip(rolled, rolled[1:])]


class Plan:
    def __init__(self, mesh, shape):
        self.sizes = {axis: mesh.shape[axis] for axis in ("gx", "gy", "gz")}
        self.nx = shape[0] // self.sizes["gx"]
        self.ny = shape[1] // self.sizes["gy"]
        self.nz = shape[2] // self.sizes["gz"]
        self.tiles = self.nz // 128
        self.rows = self.ny + 2 * HALO
        self.two_sided = self.sizes["gx"] > 2
        self.deep = self.nx + HALO * (2 if self.two_sided else 1)
        self.planes = self.deep + 2
        self.per_group = self.deep // GROUPS
        self.edge_planes = self.per_group + 2
        self.row_tiles = [OWN - HALO + 8 * t for t in range((self.ny + 2 * HALO) // 8)]
        self.own_tiles = [OWN + 8 * t for t in range(self.ny // 8)]
        self.end_tiles = [self.row_tiles[0], self.row_tiles[-1]]
        self.edge_vregs = self.per_group * len(self.row_tiles)
        self.face_vregs = -(-self.edge_vregs // 8)

    def index(self, axis):
        return lax.axis_index(axis)

    def even(self, axis):
        return lax.rem(lax.axis_index(axis), 2) == 0

    def first(self, axis):
        return lax.axis_index(axis) == 0

    def last(self, axis):
        return lax.axis_index(axis) == self.sizes[axis] - 1

    def own_plane(self):
        if self.two_sided:
            return jnp.int32(1 + HALO)
        return jnp.where(self.even("gx"), 1, 1 + HALO)

    def core(self):
        own = self.own_plane()
        if self.two_sided:
            return own + HALO, self.nx - 2 * HALO
        return own + jnp.where(self.even("gx"), 0, HALO), self.nx - HALO

    def beside(self, low, high, count):
        own = self.own_plane()
        if self.two_sided:
            return [(own + low, count), (own + high, count)]
        return [(own + jnp.where(self.even("gx"), high, low), count)]

    def strips(self, step):
        count = HALO - 1 - step
        return self.beside(step + 1, self.nx - HALO, count) if count else []

    def rims(self, step):
        return self.beside(step + 1 - HALO, self.nx - HALO, 2 * HALO - 1 - step)

    def masks(self):
        return {row: self.row_keep(row) for row in self.row_tiles + self.own_tiles}

    def row_keep(self, row):
        if row < OWN:
            return (sublanes() >= OWN - row) | jnp.logical_not(self.first("gy"))
        if row + 8 > OWN + self.ny:
            return (sublanes() < OWN + self.ny - row) | jnp.logical_not(self.last("gy"))
        return None

    def edge_keep(self):
        pos = lanes() % BLOCK
        low = (pos >= 16) & (pos < 20) & self.first("gz")
        high = (pos >= 12) & (pos < 16) & self.last("gz")
        return jnp.logical_not(low | high)


def pairs(count, second):
    if not second:
        return [(i, i ^ 1) for i in range(count)]
    inner = [(i, i + 1) for i in range(1, count - 1, 2)]
    return inner + [(b, a) for a, b in inner]


def swap(plan, axis, first, second, wrap):
    count = plan.sizes[axis]
    got = lax.ppermute(first, axis, pairs(count, False))
    if count == 2:
        return got, got
    ends = [(0, count - 1), (count - 1, 0)] if wrap else [(0, 0), (count - 1, count - 1)]
    return got, lax.ppermute(second, axis, pairs(count, True) + ends)


def send_faces(plan, fields, px, px2, pya, pyb):
    nt = plan.tiles
    own = plan.own_plane()
    even_x, even_y = plan.even("gx"), plan.even("gy")
    wide = HALO * nt
    rows = pl.ds(OWN, plan.ny)
    low, high = own * nt, (own + plan.nx - HALO) * nt
    for f, field in enumerate(fields):
        at = jnp.where(even_x, high, low)
        for j in range(wide):
            px[f * wide + j] = field[at + j, rows, :]
        if plan.two_sided:
            at = jnp.where(even_x, low, high)
            for j in range(wide):
                px2[f * wide + j] = field[at + j, rows, :]
    top = OWN + plan.ny - HALO

    def body(x, _):
        for f, field in enumerate(fields):
            for t in range(nt):
                a = field[(own + x) * nt + t, pl.ds(OWN, HALO), :]
                b = field[(own + x) * nt + t, pl.ds(top, HALO), :]
                if len(fields) == 2:
                    to = (x * nt + t, pl.ds(HALO * f, HALO))
                else:
                    to = (x * (nt // 2) + t // 2, pl.ds(HALO * (t % 2), HALO))
                pya[to[0], to[1], :] = jnp.where(even_y, b, a)
                pyb[to[0], to[1], :] = jnp.where(even_y, a, b)
        return 0

    lax.fori_loop(0, plan.nx, body, 0, unroll=4)


def corners(plan, per, ya, yb, out, out2=None):
    even = plan.even("gx")
    low, high = 0, (plan.nx - HALO) * per
    width = HALO * per
    at = jnp.where(even, high, low)
    for n, ref in enumerate((ya, yb)):
        out[n * width : (n + 1) * width] = ref[pl.ds(at, width)]
    if plan.two_sided:
        at = jnp.where(even, low, high)
        for n, ref in enumerate((ya, yb)):
            out2[n * width : (n + 1) * width] = ref[pl.ds(at, width)]


def place_halos(plan, fields, xa, xb, ya, yb, ca, cb):
    nt = plan.tiles
    own = plan.own_plane()
    wide = HALO * nt
    even_x, even_y = plan.even("gx"), plan.even("gy")
    two = len(fields) == 2
    per = nt if two else nt // 2
    below, above = own - HALO, own + plan.nx
    rows = pl.ds(OWN, plan.ny)

    def put_rows(plane, source_a, source_b, at, blank):
        for f, field in enumerate(fields):
            for t in range(nt):
                if two:
                    a = source_a[at + t, pl.ds(HALO * f, HALO), :]
                    b = source_b[at + t, pl.ds(HALO * f, HALO), :]
                else:
                    a = source_a[at + t // 2, pl.ds(HALO * (t % 2), HALO), :]
                    b = source_b[at + t // 2, pl.ds(HALO * (t % 2), HALO), :]
                low = jnp.where(even_y, b, a)
                high = jnp.where(even_y, a, b)
                low = jnp.where(plan.first("gy") | blank, 0.0, low)
                high = jnp.where(plan.last("gy") | blank, 0.0, high)
                field[plane * nt + t, pl.ds(OWN - HALO, HALO), :] = low
                field[plane * nt + t, pl.ds(OWN + plan.ny, HALO), :] = high

    def body(x, _):
        put_rows(own + x, ya, yb, x * per, False)
        return 0

    lax.fori_loop(0, plan.nx, body, 0, unroll=4)

    sides = [(xa, ca, jnp.where(even_x, above, below), False)]
    if plan.two_sided:
        sides[0] = (xa, ca, jnp.where(even_x, above, below), False)
        ends = (even_x & plan.first("gx")) | (jnp.logical_not(even_x) & plan.last("gx"))
        sides.append((xb, cb, jnp.where(even_x, below, above), ends))
    for x_ref, c_ref, plane, blank in sides:
        for f, field in enumerate(fields):
            for j in range(wide):
                value = x_ref[f * wide + j]
                if blank is not False:
                    value = jnp.where(blank, 0.0, value)
                field[plane * nt + j, rows, :] = value
        half = HALO * per
        for j in range(HALO):
            put_rows(plane + j, c_ref.at[pl.ds(0, half)], c_ref.at[pl.ds(half, half)], j * per, blank)
    zero = jnp.zeros((plan.rows, 128), F32)
    for field in fields:
        for t in range(nt):
            field[t] = zero
            field[(plan.planes - 1) * nt + t] = zero


def pack_edges(plan, field, edge, row_tiles, first, count):
    nt = plan.tiles
    masks = [lanes() >= 16 * j for j in range(2 * GROUPS)]

    for j in range(count):
        i = first + j
        for row in row_tiles:
            value = None
            for g in range(GROUPS):
                plane = (g * plan.per_group + 1 + i) * nt
                right = pltpu.roll(field[plane + nt - 1, pl.ds(row, 8), :], (BLOCK * g + 12) % 128, axis=1)
                left = pltpu.roll(field[plane, pl.ds(row, 8), :], (BLOCK * g + 20) % 128, axis=1)
                value = right if value is None else jnp.where(masks[2 * g], right, value)
                value = jnp.where(masks[2 * g + 1], left, value)
            edge[i + 1, pl.ds(row, 8), :] = value


def pack_halo_edges(plan, field, edge):
    pack_edges(plan, field, edge, plan.end_tiles, 0, plan.per_group)
    last = plan.per_group - HALO
    starts = [0, last] if plan.two_sided else [jnp.where(plan.even("gx"), last, 0)]
    for start in starts:
        pack_edges(plan, field, edge, plan.row_tiles[1:-1], start, HALO)


def edge_places(plan):
    return [(i + 1, row) for i in range(plan.per_group) for row in plan.row_tiles]


def pack_faces(plan, edge, first, second, base):
    pos = lanes() % BLOCK
    even = plan.even("gz")
    places = edge_places(plan)
    for q in range(plan.face_vregs):
        low = high = None
        for slot, (i, row) in enumerate(places[8 * q : 8 * q + 8]):
            held = edge[i, pl.ds(row, 8), :]
            a = pltpu.roll(held, (4 * slot - 20) % 128, axis=1)
            b = pltpu.roll(held, (4 * slot - 8) % 128, axis=1)
            low = a if low is None else jnp.where(pos >= 4 * slot, a, low)
            high = b if high is None else jnp.where(pos >= 4 * slot, b, high)
        first[base + q] = jnp.where(even, high, low)
        second[base + q] = jnp.where(even, low, high)


def place_faces(plan, edge, za, zb, base):
    pos = lanes() % BLOCK
    at_right, at_left = (pos >= 12) & (pos < 16), (pos >= 16) & (pos < 20)
    even = plan.even("gz")
    places = edge_places(plan)
    for q in range(plan.face_vregs):
        a, b = za[base + q], zb[base + q]
        right = jnp.where(plan.last("gz"), 0.0, jnp.where(even, a, b))
        left = jnp.where(plan.first("gz"), 0.0, jnp.where(even, b, a))
        for slot, (i, row) in enumerate(places[8 * q : 8 * q + 8]):
            value = edge[i, pl.ds(row, 8), :]
            value = jnp.where(at_right, pltpu.roll(right, (12 - 4 * slot) % 128, axis=1), value)
            value = jnp.where(at_left, pltpu.roll(left, (16 - 4 * slot) % 128, axis=1), value)
            edge[i, pl.ds(row, 8), :] = value


def wrap_planes(plan, edge):
    lane = lanes()
    last = plan.per_group
    for row in plan.row_tiles:
        before = pltpu.roll(edge[last, pl.ds(row, 8), :], BLOCK, axis=1)
        after = pltpu.roll(edge[1, pl.ds(row, 8), :], 128 - BLOCK, axis=1)
        edge[0, pl.ds(row, 8), :] = jnp.where(lane < BLOCK, 0.0, before)
        edge[last + 1, pl.ds(row, 8), :] = jnp.where(lane >= 128 - BLOCK, 0.0, after)


def merge_edges(plan, values, edge, plane, row):
    lane = lanes()
    g = (plane - 1) // plan.per_group
    i = plane - g * plan.per_group
    held = edge[i, pl.ds(row, 8), :]
    left = pltpu.roll(held, lax.rem(256 - 20 - BLOCK * g, 128), axis=1)
    right = pltpu.roll(held, lax.rem(256 - 12 - BLOCK * g, 128), axis=1)
    values = list(values)
    values[0] = jnp.where(lane < 4, left, values[0])
    values[-1] = jnp.where(lane >= 124, right, values[-1])
    return values


def face_coefficients(k, c, start, count, rows, tiles, unroll):
    cx, cy, cz, czm, *own = c

    def body(i, _):
        for row in rows:
            x = start + i * unroll
            here = load(k, x, row, tiles)
            low = add(here, load(k, x - 1, row, tiles))
            for j in range(unroll):
                x = start + i * unroll + j
                next_ = load(k, x + 1, row, tiles)
                high = add(here, next_)
                up = add(here, load(k, x, row + 1, tiles))
                down = add(here, load(k, x, row - 1, tiles))
                right, left = add(here, ahead(here)), add(here, behind(here))
                store(cx, x, row, high)
                store(cy, x, row, up)
                store(cz, x, row, right)
                store(czm, x, row, left)
                if own:
                    whole = add(add(add(low, high), add(up, down)), add(right, left))
                    store(own[0], x, row, [1.0 - value for value in whole])
                here, low = next_, high
        return 0

    repeat(body, count // unroll)


def low_faces(k, cx, plane, rows, tiles):
    for row in rows:
        store(cx, plane, row, add(load(k, plane, row, tiles), load(k, plane + 1, row, tiles)))


def repeat(body, count):
    if count == 1:
        body(0, 0)
    else:
        lax.fori_loop(0, count, body, 0)


def kept(total, mask, plane_keep, x):
    if plane_keep is not None:
        inside = plane_keep(x)
        mask = inside if mask is None else mask & inside
    if mask is None:
        return total
    return [jnp.where(mask, value, 0.0) for value in total]


def step_forward(v, w, c, start, count, rows, tiles, masks, plane_keep):
    cx, cy, cz, czm, *own = c
    for row in rows:
        before, here = load(v, start - 1, row, tiles), load(v, start, row, tiles)
        low, flow = load(cx, start - 1, row, tiles), None
        for j in range(count):
            x = start + j
            after, high = load(v, x + 1, row, tiles), load(cx, x, row, tiles)
            above, below = load(cy, x, row, tiles), load(cy, x, row - 1, tiles)
            right, left = load(cz, x, row, tiles), load(czm, x, row, tiles)
            if own:
                total = add(mul(low, before), mul(high, after))
                total = add(total, add(mul(above, load(v, x, row + 1, tiles)), mul(below, load(v, x, row - 1, tiles))))
                total = add(total, mul(load(own[0], x, row, tiles), here))
                total = add(total, add(mul(right, ahead(here)), mul(left, behind(here))))
            else:
                out = mul(high, sub(after, here))
                into = mul(low, sub(here, before)) if flow is None else flow
                flow = out
                total = add(here, sub(out, into))
                up = mul(above, sub(load(v, x, row + 1, tiles), here))
                down = mul(below, sub(here, load(v, x, row - 1, tiles)))
                total = add(total, sub(up, down))
                right, left = mul(right, sub(ahead(here), here)), mul(left, sub(here, behind(here)))
                total = add(total, sub(right, left))
            total = kept(total, masks[row], plane_keep, x)
            store(w, x, row, total)
            before, here, low = here, after, high


def step_backward(v, w, u, sums, c, start, count, rows, tiles, masks, plane_keep, unroll, fresh):
    cx, cy, cz, czm = c[:4]
    acc, az = sums

    def body(i, _):
        first = start + i * unroll
        for row in rows:
            here = load(v, first, row, tiles)
            temp = load(u, first, row, tiles)
            diff = sub(here, load(v, first - 1, row, tiles))
            flow = mul(load(cx, first - 1, row, tiles), diff)
            part = mul(diff, sub(temp, load(u, first - 1, row, tiles)))
            for k in range(unroll):
                x = first + k
                after, temp_after = load(v, x + 1, row, tiles), load(u, x + 1, row, tiles)
                diff = sub(after, here)
                out = mul(load(cx, x, row, tiles), diff)
                total = add(here, sub(out, flow))
                flow = out
                term = mul(diff, sub(temp_after, temp))
                both = add(part, term)
                part = term
                diff = sub(load(v, x, row + 1, tiles), here)
                less = sub(here, load(v, x, row - 1, tiles))
                up = mul(load(cy, x, row, tiles), diff)
                down = mul(load(cy, x, row - 1, tiles), less)
                total = add(total, sub(up, down))
                both = add(both, mul(diff, sub(load(u, x, row + 1, tiles), temp)))
                both = add(both, mul(less, sub(temp, load(u, x, row - 1, tiles))))
                store(acc, x, row, both if fresh else add(both, load(acc, x, row, tiles)))
                diff = sub(ahead(here), here)
                right = mul(load(cz, x, row, tiles), diff)
                left = mul(load(czm, x, row, tiles), sub(here, behind(here)))
                total = add(total, sub(right, left))
                term = mul(diff, sub(ahead(temp), temp))
                store(az, x, row, term if fresh else add(term, load(az, x, row, tiles)))
                total = kept(total, masks[row], plane_keep, x)
                store(w, x, row, total)
                here, temp = after, temp_after
        return 0

    repeat(body, count // unroll)


def inner_unroll(count):
    return next(n for n in (7, 6, 4, 2, 1) if count % n == 0)


def plane_keeper(plan):
    if not plan.two_sided:
        return None
    low = jnp.where(plan.first("gx"), 1 + HALO, 0)
    high = jnp.where(plan.last("gx"), 1 + HALO + plan.nx, plan.planes)
    return lambda x: (x >= low) & (x < high)


def clear_ends(plan, fields):
    zero = jnp.zeros((plan.rows, 128), F32)
    nt = plan.tiles
    for field in fields:
        for t in range(nt):
            field[t] = zero
            field[(plan.planes - 1) * nt + t] = zero


def factor_of(labels, values):
    out = jnp.zeros(labels.shape, F32) + values[0]
    for m in range(1, MATERIALS):
        out = jnp.where(labels == m, values[m], out)
    return out


def read(copies):
    for copy in copies:
        copy.start()
    for copy in copies:
        copy.wait()


def scaled(diffusivity, labels, values):
    return diffusivity * factor_of(labels, values) * HALF_RATE


def x_face_kernel(plan, scale, u0, diffusivity, labels, *refs):
    *outs, scale_s, ux, dx, lx, sems = refs
    nt = plan.tiles
    even = plan.even("gx")
    low, high = 0, plan.nx - HALO
    starts = [jnp.where(even, high, low)] + ([jnp.where(even, low, high)] if plan.two_sided else [])
    copies = [pltpu.make_async_copy(scale, scale_s, sems.at[0])]
    for s, at in enumerate(starts):
        for n, (source, held) in enumerate(((u0, ux), (diffusivity, dx), (labels, lx))):
            copies.append(pltpu.make_async_copy(source.at[pl.ds(at, HALO)], held.at[s], sems.at[1 + 3 * s + n]))
    read(copies)
    values = [scale_s[m] for m in range(MATERIALS)]
    for s, out in enumerate(outs):
        for j in range(HALO):
            for t in range(nt):
                cols = pl.ds(128 * t, 128)
                out[j * nt + t] = ux[s, j, :, cols]
                out[(HALO + j) * nt + t] = scaled(dx[s, j, :, cols], lx[s, j, :, cols], values)


def y_face_kernel(plan, scale, u0, diffusivity, labels, pya, pyb, scale_s, uy, dy, ly, sems):
    nt = plan.tiles
    even = plan.even("gy")
    copies = [pltpu.make_async_copy(scale, scale_s, sems.at[0])]
    for s, at in enumerate((0, plan.ny - 8)):
        for n, (source, held) in enumerate(((u0, uy), (diffusivity, dy), (labels, ly))):
            copies.append(pltpu.make_async_copy(source.at[:, pl.ds(at, 8), :], held.at[s], sems.at[1 + 3 * s + n]))
    read(copies)
    values = [scale_s[m] for m in range(MATERIALS)]

    def body(x, _):
        for t in range(nt):
            cols = pl.ds(128 * t, 128)
            k = [scaled(dy[s, x, :, cols], ly[s, x, :, cols], values) for s in range(2)]
            u = [uy[s, x, :, cols] for s in range(2)]
            for f, (a, b) in enumerate((u, k)):
                a, b = a[:HALO], b[8 - HALO :]
                pya[x * nt + t, pl.ds(HALO * f, HALO), :] = jnp.where(even, b, a)
                pyb[x * nt + t, pl.ds(HALO * f, HALO), :] = jnp.where(even, a, b)
        return 0

    lax.fori_loop(0, plan.nx, body, 0, unroll=4)


def own_kernel(plan, scale, u0, diffusivity, labels, u, k, *c):
    nt = plan.tiles
    own = plan.own_plane()
    values = [scale[m] for m in range(MATERIALS)]
    clear_ends(plan, (u, k))

    def body(x, _):
        for t in range(nt):
            cols = pl.ds(128 * t, 128)
            u[(own + x) * nt + t, pl.ds(OWN, plan.ny), :] = u0[x, :, cols]
            k[(own + x) * nt + t, pl.ds(OWN, plan.ny), :] = (
                scaled(diffusivity[x, :, cols], labels[x, :, cols], values)
            )
        return 0

    lax.fori_loop(0, plan.nx, body, 0, unroll=2)
    face_coefficients(k, c, own, plan.nx, plan.own_tiles, nt, 4)
    low_faces(k, c[0], own - 1, plan.own_tiles, nt)


def inner_forward_kernel(plan, steps, sources, *refs):
    c, fields = refs[:5], refs[5:]
    clear_ends(plan, fields[sources:])
    masks = dict.fromkeys(plan.own_tiles)
    start, count = plan.core()
    for n, step in enumerate(steps):
        v, w = fields[sources - 1 + n], fields[sources + n]
        step_forward(v, w, c, start, count, plan.own_tiles, plan.tiles, masks, None)
        for at, many in plan.strips(step):
            step_forward(v, w, c, at, many, plan.own_tiles, plan.tiles, masks, None)


def ready_kernel(plan, xa, xb, ya, yb, ca, cb, u_in, k_in, eu_in, ek_in, u, k, eu, ek, pza, pzb):
    del u_in, k_in, eu_in, ek_in
    place_halos(plan, (u, k), xa, xb, ya, yb, ca, cb)
    pack_halo_edges(plan, u, eu)
    pack_halo_edges(plan, k, ek)
    pack_faces(plan, eu, pza, pzb, 0)
    pack_faces(plan, ek, pza, pzb, plan.face_vregs)


def outer_forward_kernel(plan, u, k, *refs):
    c, later = refs[8:12], refs[12:]
    nt = plan.tiles
    own = plan.own_plane()
    face_coefficients(k, c, own, plan.nx, plan.end_tiles, nt, 8)
    low_faces(k, c[0], own - 1, plan.end_tiles, nt)
    for at, many in plan.beside(-HALO, plan.nx - HALO, 2 * HALO):
        face_coefficients(k, c, at, many, plan.row_tiles, nt, 4)
    fields = (u, *later)
    masks, keeper = plan.masks(), plane_keeper(plan)
    start, count = plan.core()
    for n in range(ITERS):
        step_forward(fields[n], fields[n + 1], c, start, count, plan.end_tiles, nt, masks, None)
        for at, many in plan.rims(n):
            step_forward(fields[n], fields[n + 1], c, at, many, plan.row_tiles, nt, masks, keeper)


def edge_masks(plan):
    keep = plan.edge_keep()
    return {row: keep if mask is None else keep & mask for row, mask in plan.masks().items()}


def edge_forward_kernel(plan, eu, k_in, za, zb, e0, k, u1, u2, u3, u4, *c):
    del eu, k_in
    place_faces(plan, e0, za, zb, 0)
    place_faces(plan, k, za, zb, plan.face_vregs)
    wrap_planes(plan, e0)
    wrap_planes(plan, k)
    face_coefficients(k, c, 1, plan.per_group, plan.row_tiles, 1, plan.per_group)
    low_faces(k, c[0], 0, plan.row_tiles, 1)
    masks, keeper = edge_masks(plan), edge_keeper(plan)
    fields = (e0, u1, u2, u3, u4)
    for n in range(ITERS):
        step_forward(fields[n], fields[n + 1], c, 1, plan.per_group, plan.row_tiles, 1, masks, keeper)
        if n < ITERS - 1:
            wrap_planes(plan, fields[n + 1])


def edge_keeper(plan):
    if not plan.two_sided:
        return None
    group = lanes() // BLOCK
    low = jnp.where(plan.first("gx"), plan.own_plane(), 1)
    high = jnp.where(plan.last("gx"), plan.own_plane() + plan.nx, plan.planes)

    def inside(i):
        plane = group * plan.per_group + i
        return (plane >= low) & (plane < high)

    return inside


def middle_kernel(plan, u4, e4, measured, observed, adjoint, lam, px, pya, pyb, *px2):
    nt = plan.tiles
    own = plan.own_plane()

    def body(x, _):
        for row in plan.own_tiles:
            temp = merge_edges(plan, load(u4, own + x, row, nt), e4, own + x, row)
            for t in range(nt):
                at = (x, pl.ds(row - OWN, 8), pl.ds(128 * t, 128))
                temp[t] = adjoint[at] + observed[at].astype(F32) * (temp[t] - measured[at])
            store(lam, own + x, row, temp)
        return 0

    lax.fori_loop(0, plan.nx, body, 0, unroll=4)
    clear_ends(plan, (lam,))
    send_faces(plan, (lam,), px, px2[0] if px2 else None, pya, pyb)


def inner_backward_kernel(plan, steps, fresh, given, *refs):
    c, temps = refs[:4], refs[4 : 4 + len(steps)]
    rest = refs[4 + len(steps) + given :]
    lams, sums = refs[4 + len(steps) : 5 + len(steps)] + rest[: len(steps)], rest[len(steps) :]
    clear_ends(plan, lams[1:])
    masks = dict.fromkeys(plan.own_tiles)
    start, count = plan.core()
    for n, step in enumerate(steps):
        v, w = lams[n], lams[n + 1]
        step_backward(
            v, w, temps[n], sums, c, start, count, plan.own_tiles, plan.tiles, masks, None,
            inner_unroll(count), fresh and n == 0,
        )
        for at, many in plan.strips(step):
            step_forward(v, w, c, at, many, plan.own_tiles, plan.tiles, masks, None)


def turn_kernel(plan, xa, xb, ya, yb, ca, cb, lam_in, lam, edge, pza, pzb):
    del lam_in
    place_halos(plan, (lam,), xa, xb, ya, yb, ca, cb)
    pack_edges(plan, lam, edge, plan.row_tiles, 0, plan.per_group)
    pack_faces(plan, edge, pza, pzb, 0)


def outer_backward_kernel(plan, lam, *refs):
    c, temps, rest = refs[:4], refs[4:8], refs[14:]
    later, sums = rest[:4], rest[4:]
    nt = plan.tiles
    fields = (lam, *later)
    masks, keeper = plan.masks(), plane_keeper(plan)
    start, count = plan.core()
    for m in range(ITERS):
        v, w, u = fields[m], fields[m + 1], temps[ITERS - 1 - m]
        step_backward(
            v, w, u, sums, c, start, count, plan.end_tiles, nt, masks, None, 2 * inner_unroll(count), m == 0
        )
        for at, many in plan.rims(m):
            step_backward(v, w, u, sums, c, at, many, plan.row_tiles, nt, masks, keeper, many, m == 0)


def edge_backward_kernel(plan, lam, za, zb, u0, u1, u2, u3, cx, cy, cz, czm, w, total, e, other, acc, az):
    e[...] = lam[...]
    place_faces(plan, e, za, zb, 0)
    wrap_planes(plan, e)
    masks, keeper = edge_masks(plan), edge_keeper(plan)
    fields = (u0, u1, u2, u3)
    buffers = [e, other, w, other, w]
    for m in range(ITERS):
        n = ITERS - 1 - m
        step_backward(
            buffers[m], buffers[m + 1], fields[n], (acc, az), (cx, cy, cz, czm),
            1, plan.per_group, plan.row_tiles, 1, masks, keeper, plan.per_group, m == 0,
        )
        if m < ITERS - 1:
            wrap_planes(plan, buffers[m + 1])
    for i in range(1, 1 + plan.per_group):
        for row in plan.own_tiles:
            z = [az[i, pl.ds(row, 8), :]]
            total[i, pl.ds(row, 8), :] = acc[i, pl.ds(row, 8), :] + z[0] + behind(z)[0]


def finish_kernel(plan, scale, labels, lam, acc, az, e_lam, e_total, gradient, adjoint, grad_s, adj_s, sems):
    nt = plan.tiles
    own = plan.own_plane()
    values = [scale[m] for m in range(MATERIALS)]
    chunk = 4
    count, slots = plan.nx // chunk, grad_s.shape[0]

    def copies(i):
        at, slot = pl.ds(i * chunk, chunk), lax.rem(i, slots)
        return (
            pltpu.make_async_copy(grad_s.at[slot], gradient.at[at], sems.at[0, slot]),
            pltpu.make_async_copy(adj_s.at[slot], adjoint.at[at], sems.at[1, slot]),
        )

    def drain(i):
        for copy in copies(i):
            copy.wait()

    def body(i, _):
        slot = lax.rem(i, slots)

        @pl.when(i >= slots)
        def _():
            drain(i - slots)

        for j in range(chunk):
            x = i * chunk + j
            p = own + x
            for row in plan.own_tiles:
                z = load(az, p, row, nt)
                total = add(load(acc, p, row, nt), add(z, behind(z)))
                total = merge_edges(plan, total, e_total, p, row)
                end = merge_edges(plan, load(lam, p, row, nt), e_lam, p, row)
                for t in range(nt):
                    at = (x, pl.ds(row - OWN, 8), pl.ds(128 * t, 128))
                    to = (slot, j, *at[1:])
                    grad_s[to] = total[t] * (-HALF_RATE) * factor_of(labels[at], values)
                    adj_s[to] = end[t]
        for copy in copies(i):
            copy.start()
        return 0

    lax.fori_loop(0, count, body, 0)
    for i in range(max(count - slots, 0), count):
        drain(jnp.int32(i))


def call(kernel, outs, args, alias=None, scratch=(), smem=0, flops=0, specs=None, out_spec=in_vmem, mib=3):
    if specs is None:
        specs = [in_smem] * smem + [in_vmem] * (len(args) - smem)
    cost = pl.CostEstimate(flops=flops, bytes_accessed=flops, transcendentals=0) if flops else None
    return pl.pallas_call(
        kernel,
        out_shape=tuple(outs),
        in_specs=specs,
        out_specs=(out_spec,) * len(outs),
        input_output_aliases=alias or {},
        scratch_shapes=list(scratch),
        cost_estimate=cost,
        compiler_params=params(mib),
        name=kernel.func.__name__,
    )(*args)


def shards(plan, checkpoint, diffusivity, material_scale, labels, measured, observed, adjoint_in):
    nt, nx, ny, nz = plan.tiles, plan.nx, plan.ny, plan.nz
    part = functools.partial
    work = vm(plan.planes * nt, plan.rows, 128)
    edge = vm(plan.edge_planes, plan.rows, 128)
    sides = 2 if plan.two_sided else 1

    def faces(count):
        x = vm(count * HALO * nt, ny, 128)
        y = vm(nx * nt * count // 2, 2 * HALO, 128)
        return (x, y, y) + (x,) * (sides - 1)

    def exchange(count, sent, between):
        px, pya, pyb = sent[:3]
        xa, xb = swap(plan, "gx", px, sent[-1], False)
        ya, yb = swap(plan, "gy", pya, pyb, False)
        per = nt * count // 2
        corner = vm(2 * HALO * per, 2 * HALO, 128)

        def corner_kernel(ya, yb, _, *out):
            corners(plan, per, ya, yb, *out)

        got = call(part(corner_kernel), (corner,) * sides, (ya, yb, between()))
        ca, cb = swap(plan, "gx", got[0], got[-1], False)
        return (xa, xb, ya, yb, ca, cb), got[0]

    hbm = [pltpu.with_memory_space_constraint(a, pltpu.HBM) for a in (material_scale, checkpoint, diffusivity, labels)]
    def face_call(kernel, outs, *shape):
        scratch = [pltpu.SMEM((MATERIALS,), F32), vm(*shape), vm(*shape), pltpu.VMEM(shape, jnp.int32)]
        scratch += [pltpu.SemaphoreType.DMA((1 + 3 * shape[0],))]
        return call(part(kernel, plan), outs, hbm, specs=[anywhere] * 4, mib=5, scratch=scratch)

    px, pya, pyb, *px2 = faces(2)
    px, *px2 = face_call(x_face_kernel, (px, *px2), sides, HALO, ny, nz)
    sent = (px, *face_call(y_face_kernel, (pya, pyb), 2, nx, 8, nz), *px2)
    u, k, *c = call(part(own_kernel, plan), (work,) * 7, (material_scale, checkpoint, diffusivity, labels), smem=1, flops=1 << 23)
    state = {}

    def first_half():
        state["c"], state["u"], state["new"] = c, u, call(
            part(lambda *refs: inner_forward_kernel(plan, (0, 1), 1, *refs)), (work,) * 2, (*c, u), flops=1 << 23
        )
        return state["new"][0]

    got, mark = exchange(2, sent, first_half)
    u1, u2 = state["new"]

    def later_half(mark, u, k, *refs):
        del mark
        *refs, eu, ek = refs
        inner_forward_kernel(plan, (2, 3), 1, *refs)
        pack_edges(plan, u, eu, plan.row_tiles, 0, plan.per_group)
        pack_edges(plan, k, ek, plan.row_tiles, 0, plan.per_group)

    u3, u4, eu, ek = call(part(later_half), (work, work, edge, edge), (mark, u, k, *c, u2), flops=1 << 23)
    lanes_sent = vm(2 * plan.face_vregs, 8, 128)
    u, k, eu, ek, pza, pzb = call(
        part(after(ready_kernel), plan), (work, work, edge, edge, lanes_sent, lanes_sent),
        (u4, *got, u, k, eu, ek), alias={7 + i: i for i in range(4)},
    )
    za, zb = swap(plan, "gz", pza, pzb, True)
    out = call(
        part(outer_forward_kernel, plan), (work,) * 8, (u, k, *c[:4], u1, u2, u3, u4),
        alias={2 + i: i for i in range(8)}, flops=1 << 24,
    )
    c, (u1, u2, u3, u4) = out[:4], out[4:]
    e0, _, e1, e2, e3, e4, ex, ey, ez, ezm, _ = call(
        part(edge_forward_kernel, plan), (edge,) * 11, (eu, ek, za, zb), alias={0: 0, 1: 1}
    )
    lam, *sent = call(
        part(middle_kernel, plan), (work,) + faces(1), (u4, e4, measured, observed, adjoint_in), alias={0: 0}
    )

    def first_back():
        state["new"] = call(
            part(lambda *refs: inner_backward_kernel(plan, (0, 1), True, 1, *refs)), (work,) * 4,
            (*c, u3, u2, lam), flops=1 << 24,
        )
        return state["new"][0]

    got, mark = exchange(1, sent, first_back)
    l3, l2, acc, az = state["new"]

    def later_back(mark, *refs):
        del mark
        inner_backward_kernel(plan, (2, 3), False, 3, *refs)

    l1, l0, acc, az = call(
        part(later_back), (work,) * 4, (mark, *c, u1, u, l2, acc, az), alias={8: 2, 9: 3}, flops=1 << 24
    )
    lanes_sent = vm(plan.face_vregs, 8, 128)
    lam, e_lam, pza, pzb = call(
        part(after(turn_kernel), plan), (work, edge, lanes_sent, lanes_sent), (l0, *got, lam), alias={7: 0}
    )
    za, zb = swap(plan, "gz", pza, pzb, True)
    l3, l2, l1, l0, acc, az = call(
        part(outer_backward_kernel, plan), (work,) * 6, (lam, *c, u, u1, u2, u3, l3, l2, l1, l0, acc, az),
        alias={9 + i: i for i in range(6)}, flops=1 << 25,
    )
    e_start, e_total = call(
        part(edge_backward_kernel, plan), (edge,) * 2, (e_lam, za, zb, e0, e1, e2, e3, ex, ey, ez, ezm), scratch=(edge,) * 4
    )
    block = jax.ShapeDtypeStruct((nx, ny, nz), F32)
    return call(
        part(finish_kernel, plan), (block, block), (material_scale, labels, l0, acc, az, e_start, e_total), smem=1,
        out_spec=anywhere, mib=4, scratch=[vm(4, 4, ny, nz), vm(4, 4, ny, nz), pltpu.SemaphoreType.DMA((2, 4))],
    )


def after(kernel):
    @functools.wraps(kernel)
    def waiting(plan, _, *refs):
        kernel(plan, *refs)

    return waiting


def solution(mesh):
    spec = P("gx", "gy", "gz")

    def run(*args):
        plan = Plan(mesh, args[0].shape)
        return jax.shard_map(
            functools.partial(shards, plan),
            mesh=mesh,
            in_specs=(spec, spec, P(), spec, spec, spec, spec),
            out_specs=(spec, spec),
            check_vma=False,
        )(*args)

    return run
```
